512 devices in a mesh: dp: 8 (over x, core), space: 16 (over y, z_hi), mp: 4 (over z_lo).
Axes of the slice: x: 4, y: 8, z: 8 (z_hi: 2, z_lo: 4; z = z_hi * 4 + z_lo), core: 2. Of those that a mesh axis runs over, the one named last changes fastest.
Arguments:
- teacher_tokens: bfloat16 [64, 16, 16, 16, 1408], P('dp', 'space'), parts along dimension 0, may hold values from -16 to 16
- student_tokens: bfloat16 [64, 16, 16, 16, 1280], P('dp', 'space'), parts along dimension 0, may hold values from -16 to 16
- teacher_head: bfloat16 [11264, 1000], P(('dp', 'space'), 'mp'), parts along dimension 0, may hold values from -1 to 1
- student_head: bfloat16 [10240, 1000], P(('dp', 'space'), 'mp'), parts along dimension 0, may hold values from -1 to 1
- valid: int32 [64, 16, 16, 16], P('dp', 'space'), parts along dimension 0, may hold values from 0 to 1, as said below
Outputs:
- patch_kl: float32 [64, 16, 16, 16], P('dp', 'space'), parts along dimension 0
- image_loss: float32 [64], P('dp'), parts along dimension 0
The draws below stay inside these ranges and needn't reach their ends.
There are 8 independent parts, one for each index of `dp`. The reference program is written for one: setup_inputs(seed, part) draws one part's arguments, and reference() takes and returns one part's arrays. A program takes and returns all parts, laid end to end along the dimension named above; each array names one. Nothing has to cross between parts.
Inputs may be any that keep to these rules, and one draw needn't show every extreme that they name: An image may have no valid patch.
All inputs are finite; a program needn't handle non-finite values.
Results may differ from the reference program's by a relative error of at most 0.0003.
Values may be sent and summed in bfloat16 or wider, within the bound.
No kernel may reach another device: no remote copies, remote signals or barrier semaphores. Data moves between devices by JAX's collectives and lax.ppermute only.
A program may use at most 64 MiB of HBM per device.

```python
import math
import jax
import jax.numpy as jnp
from jax import lax

TEACHER_WIDTH = 1408
STUDENT_WIDTH = 1280
CLASSES = 1000
IMAGES = 8
TILE_SIDE = 16
TILES = 16


def head_matrix(key, width, salt):
    values = jax.random.normal(jax.random.fold_in(key, salt), (width, CLASSES), jnp.float32)
    return jnp.clip(values * (3.0 / math.sqrt(width)), -1.0, 1.0)


def token_field(key, width, salt):
    base = jax.random.normal(jax.random.fold_in(key, salt + 1), (IMAGES, TILES, TILE_SIDE, TILE_SIDE, width), jnp.float32)
    base = jnp.clip(base, -6.0, 6.0)
    return base.astype(jnp.bfloat16)


def draw_teacher_tokens(key, part):
    return token_field(key, TEACHER_WIDTH, 100)


def draw_student_tokens(key, part):
    return token_field(key, STUDENT_WIDTH, 200)


def draw_teacher_head(key, part):
    return head_matrix(key, TEACHER_WIDTH, 100).astype(jnp.bfloat16)


def draw_student_head(key, part):
    return head_matrix(key, STUDENT_WIDTH, 200).astype(jnp.bfloat16)


def draw_valid(key, part):
    levels = jax.random.randint(jax.random.fold_in(key, 300), (IMAGES, TILES, TILE_SIDE, TILE_SIDE), 0, 4)
    marks = (levels < 3).astype(jnp.int32)
    image_number = jnp.arange(IMAGES)[:, None, None, None]
    empty = (image_number == IMAGES - 1) & (part % 4 == 3)
    return jnp.where(empty, jnp.zeros_like(marks), marks).astype(jnp.int32)


def setup_inputs(seed: int = 0, part: int = 0) -> dict:
    key_list = jax.random.split(jax.random.key(seed), 6)
    own_keys = jax.random.split(jax.random.fold_in(key_list[5], part), 6)
    return {
        "teacher_tokens": draw_teacher_tokens(jax.random.fold_in(jax.random.fold_in(key_list[5], part), 71), part),
        "student_tokens": draw_student_tokens(jax.random.fold_in(jax.random.fold_in(key_list[5], part), 71), part),
        "teacher_head": draw_teacher_head(jax.random.fold_in(jax.random.fold_in(key_list[5], part), 71), part),
        "student_head": draw_student_head(jax.random.fold_in(jax.random.fold_in(key_list[5], part), 71), part),
        "valid": draw_valid(jax.random.fold_in(jax.random.fold_in(key_list[5], part), 71), part),
    }


def to_grid(x):
    side = math.isqrt(TILES)
    shaped = x.reshape((IMAGES, side, side, TILE_SIDE, TILE_SIDE) + x.shape[4:])
    shaped = jnp.swapaxes(shaped, 2, 3)
    return shaped.reshape((IMAGES, side * TILE_SIDE, side * TILE_SIDE) + x.shape[4:])

def to_tiles(x):
    side = math.isqrt(TILES)
    shaped = x.reshape((IMAGES, side, TILE_SIDE, side, TILE_SIDE) + x.shape[3:])
    shaped = jnp.swapaxes(shaped, 2, 3)
    return shaped.reshape((IMAGES, TILES, TILE_SIDE, TILE_SIDE) + x.shape[3:])

def smooth(logits):
    extent = logits.shape[1]
    padded = jnp.pad(logits, ((0, 0), (1, 1), (1, 1), (0, 0)))
    total = jnp.zeros_like(logits)
    for shift_y in range(3):
        for shift_x in range(3):
            total = total + padded[:, shift_y:shift_y + extent, shift_x:shift_x + extent, :]
    ones = jnp.pad(jnp.ones((extent,), jnp.float32), 1)
    line = ones[:-2] + ones[1:-1] + ones[2:]
    count = line[:, None] * line[None, :]
    return total / count[None, :, :, None]

def reference(teacher_tokens, student_tokens, teacher_head, student_head, valid):
    teacher_grid = to_grid(teacher_tokens)
    student_grid = to_grid(student_tokens)
    extent = teacher_grid.shape[1]
    teacher_logits = jnp.dot(teacher_grid.reshape(-1, TEACHER_WIDTH), teacher_head, preferred_element_type=jnp.float32)
    student_logits = jnp.dot(student_grid.reshape(-1, STUDENT_WIDTH), student_head, preferred_element_type=jnp.float32)
    teacher_logits = teacher_logits.reshape(IMAGES, extent, extent, CLASSES)
    student_logits = student_logits.reshape(IMAGES, extent, extent, CLASSES)
    smoothed = smooth(teacher_logits)
    teacher_logp = jax.nn.log_softmax(smoothed, axis=-1)
    student_logp = jax.nn.log_softmax(student_logits, axis=-1)
    divergence = lax.optimization_barrier(jnp.sum(jnp.exp(teacher_logp) * (teacher_logp - student_logp), axis=-1))
    weights = to_grid(valid).astype(jnp.float32)
    totals = lax.optimization_barrier(jnp.sum(divergence * weights, axis=(1, 2)))
    counts = lax.optimization_barrier(jnp.sum(weights, axis=(1, 2)))
    image_loss = totals / jnp.maximum(counts, 1.0)
    return (to_tiles(divergence), image_loss)
```

```python
import math

import jax
import jax.numpy as jnp
from jax import lax
from jax.experimental import pallas as pl
from jax.experimental.pallas import tpu as pltpu
from jax.sharding import PartitionSpec as P

F32 = jnp.float32


def copies(x, count):
    return jnp.broadcast_to(x, (count, *x.shape))


def exchange(x, axis):
    return lax.all_to_all(x, axis, split_axis=0, concat_axis=0, tiled=True)


def gathered_rows(x, axis):
    everyone = exchange(copies(x, lax.axis_size(axis)), axis)
    return everyone.reshape(-1, x.shape[-1])


def shifted(block, axis, distance):
    devices = range(lax.axis_size(axis))
    route = [(i - distance, i) for i in devices if i - distance in devices]
    return lax.ppermute(block, axis, route)


def column_route(distance, side):
    route = []
    for i in range(side * side):
        if 0 <= i % side + distance < side:
            route.append((i, i + distance))
    return route


def teacher_kernel(edge, tokens_ref, head_ref, logits_ref, first_ref, last_ref, left_ref, right_ref):
    tokens = tokens_ref[0, 0].reshape(edge * edge, tokens_ref.shape[-1])
    logits = jnp.dot(tokens, head_ref[...], preferred_element_type=F32)
    logits_ref[0] = logits
    first_ref[0] = logits[:edge]
    last_ref[0] = logits[-edge:]
    cube = logits.reshape(edge, edge, logits.shape[-1])
    left_ref[0] = cube[:, 0, :]
    right_ref[0] = cube[:, edge - 1, :]


def teacher_logits(tokens, head):
    images, _, edge, _, width = tokens.shape
    classes = head.shape[1]
    line = pl.BlockSpec((1, edge, classes), lambda i: (i, 0, 0))
    border = jax.ShapeDtypeStruct((images, edge, classes), F32)
    patches = edge * edge
    return pl.pallas_call(
        lambda *refs: teacher_kernel(edge, *refs),
        grid=(images,),
        in_specs=[
            pl.BlockSpec((1, 1, edge, edge, width), lambda i: (i, 0, 0, 0, 0)),
            pl.BlockSpec((width, classes), lambda i: (0, 0)),
        ],
        out_specs=[pl.BlockSpec((1, patches, classes), lambda i: (i, 0, 0))] + [line] * 4,
        out_shape=[jax.ShapeDtypeStruct((images, patches, classes), F32)] + [border] * 4,
        compiler_params=pltpu.CompilerParams(vmem_limit_bytes=16 * 2**20),
        cost_estimate=pl.CostEstimate(
            flops=2 * images * patches * width * classes,
            bytes_accessed=tokens.size * 2 + head.size * 2 + images * patches * classes * 4,
            transcendentals=0,
        ),
        name="teacher_logits",
    )(tokens, head)


def stats_kernel(
    edge, parts, images, place_ref, tokens_ref, head_ref, logits_ref, up_ref, down_ref, left_ref, right_ref, out_ref
):
    image = pl.program_id(0)
    patches = edge * edge
    classes = head_ref.shape[1]
    tokens = tokens_ref[0, 0].reshape(patches, tokens_ref.shape[-1])
    student = jnp.dot(tokens, head_ref[...], preferred_element_type=F32)

    cube = logits_ref[0].reshape(edge, edge, classes)
    above = jnp.concatenate([up_ref[...], cube[:-1]], axis=0)
    below = jnp.concatenate([cube[1:], down_ref[...]], axis=0)
    columns = above + cube + below
    flat = columns.reshape(patches, classes)
    shape = (edge, edge, classes)
    x = lax.broadcasted_iota(jnp.int32, shape, 1)
    to_left = jnp.broadcast_to(left_ref[0][:, None, :], shape)
    to_right = jnp.broadcast_to(right_ref[0][:, None, :], shape)
    before = jnp.where(x == 0, to_left, pltpu.roll(flat, 1, 0).reshape(shape))
    after = jnp.where(x == edge - 1, to_right, pltpu.roll(flat, patches - 1, 0).reshape(shape))
    total = columns + before + after

    extent = place_ref[2]
    place_y = place_ref[0] + lax.broadcasted_iota(jnp.int32, (edge, edge, 1), 0)
    place_x = place_ref[1] + lax.broadcasted_iota(jnp.int32, (edge, edge, 1), 1)

    def line(place):
        return 1.0 + (place > 0).astype(F32) + (place < extent - 1).astype(F32)

    share = 1.0 / (line(place_y) * line(place_x))
    smoothed = (total * share).reshape(patches, classes)

    top_t = jnp.max(smoothed, axis=-1, keepdims=True)
    expo_t = jnp.exp(smoothed - top_t)
    sum_t = jnp.sum(expo_t, axis=-1, keepdims=True)
    gap = jnp.sum(expo_t * (smoothed - student), axis=-1, keepdims=True)
    top_s = jnp.max(student, axis=-1, keepdims=True)
    sum_s = jnp.sum(jnp.exp(student - top_s), axis=-1, keepdims=True)

    lane = lax.broadcasted_iota(jnp.int32, (patches, 128), 1)
    packed = jnp.where(lane == 0, top_t, jnp.where(lane == 1, sum_t, gap))
    packed = jnp.where(lane == 3, top_s, jnp.where(lane == 4, sum_s, packed))
    rows = packed.T
    top_t, sum_t, gap, top_s, sum_s = (rows[k : k + 1] for k in range(5))
    stats = (top_t + jnp.log(sum_t), gap / sum_t, top_s + jnp.log(sum_s))
    for k, stat in enumerate(stats):
        for c in range(parts):
            out_ref[c, pl.ds(k * images + image, 1), :] = stat


def patch_stats(place, tokens, head, logits, up, down, left, right, parts):
    images, _, edge, _, width = tokens.shape
    classes = head.shape[1]
    patches = edge * edge
    line = pl.BlockSpec((1, edge, classes), lambda i: (i, 0, 0))
    return pl.pallas_call(
        lambda *refs: stats_kernel(edge, parts, images, *refs),
        grid=(images,),
        in_specs=[
            pl.BlockSpec(memory_space=pltpu.SMEM),
            pl.BlockSpec((1, 1, edge, edge, width), lambda i: (i, 0, 0, 0, 0)),
            pl.BlockSpec((width, classes), lambda i: (0, 0)),
            pl.BlockSpec((1, patches, classes), lambda i: (i, 0, 0)),
            line,
            line,
            line,
            line,
        ],
        out_specs=pl.BlockSpec((parts, 3 * images, patches), lambda i: (0, 0, 0)),
        out_shape=jax.ShapeDtypeStruct((parts, 3 * images, patches), F32),
        compiler_params=pltpu.CompilerParams(vmem_limit_bytes=24 * 2**20),
        cost_estimate=pl.CostEstimate(
            flops=2 * images * patches * width * classes,
            bytes_accessed=tokens.size * 2 + head.size * 2 + images * patches * classes * 4,
            transcendentals=2 * images * patches * classes,
        ),
        name="patch_stats",
    )(place, tokens, head, logits, up, down, left, right)


def divergence_kernel(images, tiles, stats_ref, valid_ref, divergence_ref, totals_ref):
    lse_t = stats_ref[:, :images, :]
    gap = stats_ref[:, images : 2 * images, :]
    lse_s = stats_ref[:, 2 * images :, :]
    top_t = jnp.max(lse_t, axis=0)
    top_s = jnp.max(lse_s, axis=0)
    share = jnp.exp(lse_t - top_t[None])
    sum_t = jnp.sum(share, axis=0)
    sum_s = jnp.sum(jnp.exp(lse_s - top_s[None]), axis=0)
    mean_gap = jnp.sum(share * gap, axis=0) / sum_t
    divergence = mean_gap - top_t - jnp.log(sum_t) + top_s + jnp.log(sum_s)
    divergence_ref[...] = divergence
    weights = valid_ref[...].astype(F32)
    total = jnp.sum(divergence * weights, axis=1, keepdims=True)
    number = jnp.sum(weights, axis=1, keepdims=True)
    shape = (images, 128)
    lane = lax.broadcasted_iota(jnp.int32, shape, 1)
    row = lax.broadcasted_iota(jnp.int32, shape, 0)
    both = jnp.where(lane == row, total, jnp.where(lane == row + images, number, 0.0))
    line = jnp.sum(both, axis=0, keepdims=True)
    totals_ref[...] = jnp.broadcast_to(line[None], totals_ref.shape)


def patch_divergence(stats, valid, tiles):
    images, patches = valid.shape
    whole = pl.BlockSpec(memory_space=pltpu.VMEM)
    return pl.pallas_call(
        lambda *refs: divergence_kernel(images, tiles, *refs),
        in_specs=[whole, whole],
        out_specs=[whole, whole],
        out_shape=[
            jax.ShapeDtypeStruct((images, patches), F32),
            jax.ShapeDtypeStruct((tiles, 1, 128), F32),
        ],
        compiler_params=pltpu.CompilerParams(vmem_limit_bytes=8 * 2**20),
        name="patch_divergence",
    )(stats, valid)


def summed_columns(column, above, below):
    tall = jnp.concatenate([above, column, below], axis=1)
    return tall[:, :-2] + tall[:, 1:-1] + tall[:, 2:]


def body(teacher_tokens, student_tokens, teacher_head, student_head, valid):
    tiles = lax.axis_size("space")
    parts = lax.axis_size("mp")
    side = math.isqrt(tiles)
    tile_index = lax.axis_index("space")
    images, _, edge, _, _ = teacher_tokens.shape
    place = jnp.stack([tile_index // side * edge, tile_index % side * edge, side * edge]).astype(jnp.int32)
    flags = valid.reshape(images, edge * edge)

    head_t = gathered_rows(teacher_head, "space")
    head_s = gathered_rows(student_head, "space")
    logits, first, last, left_edge, right_edge = teacher_logits(teacher_tokens, head_t)
    up = shifted(last, "space", side)
    down = shifted(first, "space", -side)
    left_edge = summed_columns(left_edge, up[:, :1], down[:, :1])
    right_edge = summed_columns(right_edge, up[:, -1:], down[:, -1:])
    left = lax.ppermute(right_edge, "space", column_route(1, side))
    right = lax.ppermute(left_edge, "space", column_route(-1, side))
    stats = patch_stats(place, student_tokens, head_s, logits, up, down, left, right, parts)
    stats = exchange(stats, "mp")
    divergence, totals = patch_divergence(stats, flags, tiles)
    totals = jnp.sum(exchange(totals, "space"), axis=(0, 1))
    image_loss = totals[:images] / jnp.maximum(totals[images : 2 * images], 1.0)
    return (divergence.reshape(images, 1, edge, edge), image_loss)


def solution(mesh):
    in_specs = (
        P("dp", "space", None, None, None),
        P("dp", "space", None, None, None),
        P(("dp", "space"), "mp"),
        P(("dp", "space"), "mp"),
        P("dp", "space", None, None),
    )
    out_specs = (P("dp", "space", None, None), P("dp"))
    return jax.shard_map(body, mesh=mesh, in_specs=in_specs, out_specs=out_specs, check_vma=False)
```

```python
import math

import jax
import jax.numpy as jnp
from jax import lax
from jax.experimental import pallas as pl
from jax.experimental.pallas import tpu as pltpu
from jax.sharding import PartitionSpec as P

F32 = jnp.float32
LANES = 256


def copies(x, count):
    return jnp.broadcast_to(x, (count, *x.shape))


def exchange(x, axis):
    return lax.all_to_all(x, axis, split_axis=0, concat_axis=0, tiled=True)


def gathered_heads(teacher_head, student_head, tiles):
    classes = teacher_head.shape[1]
    own = jnp.concatenate([teacher_head, student_head])
    own = jnp.pad(own, ((0, 0), (0, LANES - classes)))
    other = lax.ppermute(own, "space", [(t, t ^ 1) for t in range(tiles)])
    first = lax.axis_index("space") % 2 == 0
    even, odd = jnp.where(first, own, other), jnp.where(first, other, own)
    cut = teacher_head.shape[0]
    pair = jnp.concatenate([even[:cut], odd[:cut], even[cut:], odd[cut:]])
    groups = [list(range(z, tiles, 2)) for z in range(2)]
    return lax.all_gather(pair, "space", axis_index_groups=groups)


def swapped(block, pairs, parts, shift):
    route = []
    for a, b in pairs:
        for m in range(parts):
            n = (m + shift) % parts
            route += [(a * parts + m, b * parts + n), (b * parts + n, a * parts + m)]
    return lax.ppermute(block, ("space", "mp"), route)


def pairs_of(side, start, down, right):
    pairs = []
    for row in range(side):
        for column in range(side):
            place = row * down + column * right
            if place % 2 == start and place + 1 < side:
                here = row * side + column
                pairs.append((here, here + down * side + right))
    return pairs


def border_tokens(tokens, side, row, column, parts):
    images, edge, _, width = tokens.shape
    row_even, column_even = row % 2 == 0, column % 2 == 0
    last, none = edge - 1, 0

    def near(even):
        return jnp.where(even, last, none), jnp.where(even, none, last)

    rows = [
        swapped(lax.dynamic_index_in_dim(tokens, y, 1, keepdims=False), pairs_of(side, k, 1, 0), parts, 0)
        for k, y in enumerate(near(row_even))
    ]
    columns = []
    for k, x in enumerate(near(column_even)):
        own = lax.dynamic_index_in_dim(tokens, x, 2, keepdims=False)
        ends = [lax.dynamic_index_in_dim(r, x, 1, keepdims=False) for r in rows]
        top, bottom = jnp.where(row_even, ends[1], ends[0]), jnp.where(row_even, ends[0], ends[1])
        line = jnp.concatenate([own.reshape(images * edge, width), top, bottom])
        columns.append(swapped(line, pairs_of(side, k, 0, 1), parts, parts // 2))
    return [r.reshape(images * edge, width) for r in rows] + columns


def in_lanes(columns):
    height = columns[0].shape[0]
    lane = lax.broadcasted_iota(jnp.int32, (height, 128), 1)
    packed = jnp.broadcast_to(columns[-1], (height, 128))
    for k, column in enumerate(columns[:-1]):
        packed = jnp.where(lane == k, column, packed)
    rows = packed.T
    return [rows[k : k + 1] for k in range(len(columns))]


def stats_kernel(
    edge,
    classes,
    parts,
    images,
    place_ref,
    teacher_ref,
    student_ref,
    heads_ref,
    row_refs,
    column_refs,
    out_ref,
    teacher_head,
    student_head,
    rows_out,
    columns_out,
):
    image = pl.program_id(0)
    patches = edge * edge
    shape = (edge, edge, LANES)

    @pl.when(image == 0)
    def _():
        pairs = heads_ref.shape[0]
        cut = teacher_head.shape[0] // pairs
        rest = student_head.shape[0] // pairs
        for k in range(pairs):
            teacher_head[k * cut : (k + 1) * cut, :] = heads_ref[k, :cut, :]
            student_head[k * rest : (k + 1) * rest, :] = heads_ref[k, cut:, :]
        for refs, out, even in ((row_refs, rows_out, place_ref[3]), (column_refs, columns_out, place_ref[4])):
            for k, ref in enumerate(refs):
                after = even if k == 0 else 1 - even
                out[after] = jnp.dot(ref[...], teacher_head[...], preferred_element_type=F32)

    tokens = teacher_ref[0, 0].reshape(patches, teacher_ref.shape[-1])
    teacher = jnp.dot(tokens, teacher_head[...], preferred_element_type=F32)
    tokens = student_ref[0, 0].reshape(patches, student_ref.shape[-1])
    student = jnp.dot(tokens, student_head[...], preferred_element_type=F32)

    here = pl.ds(pl.multiple_of(image * edge, edge), edge)
    cube = teacher.reshape(shape)
    above = jnp.concatenate([rows_out[0, here, :][None], cube[:-1]], axis=0)
    below = jnp.concatenate([cube[1:], rows_out[1, here, :][None]], axis=0)
    columns = above + cube + below
    flat = columns.reshape(patches, LANES)

    y = lax.broadcasted_iota(jnp.int32, (edge, LANES), 0)

    def side_column(side):
        line = columns_out[side, here, :]
        top = columns_out[side, pl.ds(images * edge + image, 1), :]
        bottom = columns_out[side, pl.ds(images * edge + images + image, 1), :]
        over = jnp.where(y == 0, top, pltpu.roll(line, 1, 0))
        under = jnp.where(y == edge - 1, bottom, pltpu.roll(line, edge - 1, 0))
        return jnp.broadcast_to((line + over + under)[:, None, :], shape)

    x = lax.broadcasted_iota(jnp.int32, shape, 1)
    before = jnp.where(x == 0, side_column(0), pltpu.roll(flat, 1, 0).reshape(shape))
    after = jnp.where(x == edge - 1, side_column(1), pltpu.roll(flat, patches - 1, 0).reshape(shape))
    total = columns + before + after

    extent = place_ref[2]
    place_y = place_ref[0] + lax.broadcasted_iota(jnp.int32, (edge, edge, 1), 0)
    place_x = place_ref[1] + lax.broadcasted_iota(jnp.int32, (edge, edge, 1), 1)

    def line(place):
        return 1.0 + (place > 0).astype(F32) + (place < extent - 1).astype(F32)

    share = 1.0 / (line(place_y) * line(place_x))
    smoothed = (total * share).reshape(patches, LANES)[:, :classes]
    student = student[:, :classes]

    top_t = jnp.max(smoothed, axis=-1, keepdims=True)
    expo_t = jnp.exp(smoothed - top_t)
    sum_t = jnp.sum(expo_t, axis=-1, keepdims=True)
    gap = jnp.sum(expo_t * (smoothed - student), axis=-1, keepdims=True)
    top_s = jnp.max(student, axis=-1, keepdims=True)
    sum_s = jnp.sum(jnp.exp(student - top_s), axis=-1, keepdims=True)
    top_t, sum_t, gap, top_s, sum_s = in_lanes([top_t, sum_t, gap, top_s, sum_s])
    stats = (top_t + jnp.log(sum_t), gap / sum_t, top_s + jnp.log(sum_s))
    for k, stat in enumerate(stats):
        for c in range(parts):
            out_ref[c, pl.ds(k * images + image, 1), :] = stat


def patch_stats(place, teacher, student, heads, borders, classes, parts):
    images, _, edge, _, width_t = teacher.shape
    width_s = student.shape[-1]
    patches = edge * edge

    def kernel(place_ref, teacher_ref, student_ref, heads_ref, a, b, c, d, out_ref, *scratch):
        stats_kernel(
            edge, classes, parts, images, place_ref, teacher_ref, student_ref, heads_ref, (a, b), (c, d), out_ref, *scratch
        )

    def tile(width):
        return pl.BlockSpec((1, 1, edge, edge, width), lambda i: (i, 0, 0, 0, 0))

    def whole(x):
        return pl.BlockSpec(x.shape, lambda i: (0,) * x.ndim)

    return pl.pallas_call(
        kernel,
        grid=(images,),
        in_specs=[
            pl.BlockSpec(memory_space=pltpu.SMEM),
            tile(width_t),
            tile(width_s),
            whole(heads),
            *[whole(b) for b in borders],
        ],
        out_specs=pl.BlockSpec((parts, 3 * images, patches), lambda i: (0, 0, 0)),
        out_shape=jax.ShapeDtypeStruct((parts, 3 * images, patches), F32),
        scratch_shapes=[
            pltpu.VMEM((width_t, LANES), heads.dtype),
            pltpu.VMEM((width_s, LANES), heads.dtype),
            pltpu.VMEM((2, borders[0].shape[0], LANES), F32),
            pltpu.VMEM((2, borders[2].shape[0], LANES), F32),
        ],
        compiler_params=pltpu.CompilerParams(vmem_limit_bytes=24 * 2**20),
        cost_estimate=pl.CostEstimate(
            flops=2 * images * patches * (width_t + width_s) * LANES,
            bytes_accessed=(teacher.size + student.size + heads.size) * 2,
            transcendentals=2 * images * patches * LANES,
        ),
        name="patch_stats",
    )(place, teacher, student, heads, *borders)


def divergence_kernel(images, tiles, stats_ref, valid_ref, divergence_ref, totals_ref):
    lse_t = stats_ref[:, :images, :]
    gap = stats_ref[:, images : 2 * images, :]
    lse_s = stats_ref[:, 2 * images :, :]
    top_t = jnp.max(lse_t, axis=0)
    top_s = jnp.max(lse_s, axis=0)
    share = jnp.exp(lse_t - top_t[None])
    sum_t = jnp.sum(share, axis=0)
    sum_s = jnp.sum(jnp.exp(lse_s - top_s[None]), axis=0)
    mean_gap = jnp.sum(share * gap, axis=0) / sum_t
    divergence = mean_gap - top_t - jnp.log(sum_t) + top_s + jnp.log(sum_s)
    divergence_ref[...] = divergence
    weights = valid_ref[...].astype(F32)
    total = jnp.sum(divergence * weights, axis=1, keepdims=True)
    number = jnp.sum(weights, axis=1, keepdims=True)
    shape = (images, 128)
    lane = lax.broadcasted_iota(jnp.int32, shape, 1)
    row = lax.broadcasted_iota(jnp.int32, shape, 0)
    both = jnp.where(lane == row, total, jnp.where(lane == row + images, number, 0.0))
    line = jnp.sum(both, axis=0, keepdims=True)
    totals_ref[...] = jnp.broadcast_to(line[None], totals_ref.shape)


def patch_divergence(stats, valid, tiles):
    images, patches = valid.shape
    whole = pl.BlockSpec(memory_space=pltpu.VMEM)
    return pl.pallas_call(
        lambda *refs: divergence_kernel(images, tiles, *refs),
        in_specs=[whole, whole],
        out_specs=[whole, whole],
        out_shape=[
            jax.ShapeDtypeStruct((images, patches), F32),
            jax.ShapeDtypeStruct((tiles, 1, 128), F32),
        ],
        compiler_params=pltpu.CompilerParams(vmem_limit_bytes=8 * 2**20),
        name="patch_divergence",
    )(stats, valid)


def everywhere_sum(x, tiles, parts):
    groups = []
    for start in range(parts):
        groups.append([t * parts + (start + t % 2 * (parts // 2)) % parts for t in range(tiles)])
    everyone = lax.all_to_all(
        x, ("space", "mp"), split_axis=0, concat_axis=0, tiled=True, axis_index_groups=groups
    )
    return jnp.sum(everyone, axis=(0, 1))


def body(teacher_tokens, student_tokens, teacher_head, student_head, valid):
    tiles = lax.axis_size("space")
    parts = lax.axis_size("mp")
    side = math.isqrt(tiles)
    tile_index = lax.axis_index("space")
    row, column = tile_index // side, tile_index % side
    images, _, edge, _, _ = teacher_tokens.shape
    flags = valid.reshape(images, edge * edge)
    place = jnp.stack([row * edge, column * edge, side * edge, 1 - row % 2, 1 - column % 2]).astype(jnp.int32)

    heads = gathered_heads(teacher_head, student_head, tiles)
    borders = border_tokens(teacher_tokens[:, 0], side, row, column, parts)
    stats = patch_stats(place, teacher_tokens, student_tokens, heads, borders, teacher_head.shape[1], parts)
    stats = exchange(stats, "mp")
    divergence, totals = patch_divergence(stats, flags, tiles)
    totals = everywhere_sum(totals, tiles, parts)
    image_loss = totals[:images] / jnp.maximum(totals[images : 2 * images], 1.0)
    return (divergence.reshape(images, 1, edge, edge), image_loss)


def solution(mesh):
    in_specs = (
        P("dp", "space", None, None, None),
        P("dp", "space", None, None, None),
        P(("dp", "space"), "mp"),
        P(("dp", "space"), "mp"),
        P("dp", "space", None, None),
    )
    out_specs = (P("dp", "space", None, None), P("dp"))
    return jax.shard_map(body, mesh=mesh, in_specs=in_specs, out_specs=out_specs, check_vma=False)
```

```python
import math

import jax
import jax.numpy as jnp
from jax import lax
from jax.experimental import pallas as pl
from jax.experimental.pallas import tpu as pltpu
from jax.sharding import PartitionSpec as P

F32 = jnp.float32
LANES = 256


def copies(x, count):
    return jnp.broadcast_to(x, (count, *x.shape))


def exchange(x, axis):
    return lax.all_to_all(x, axis, split_axis=0, concat_axis=0, tiled=True)


def gathered_heads(teacher_head, student_head, tiles):
    classes = teacher_head.shape[1]
    own = jnp.concatenate([teacher_head, student_head])
    own = jnp.pad(own, ((0, 0), (0, LANES - classes)))
    other = lax.ppermute(own, "space", [(t, t ^ 1) for t in range(tiles)])
    first = lax.axis_index("space") % 2 == 0
    even, odd = jnp.where(first, own, other), jnp.where(first, other, own)
    cut = teacher_head.shape[0]
    pair = jnp.concatenate([even[:cut], odd[:cut], even[cut:], odd[cut:]])
    groups = [list(range(z, tiles, 2)) for z in range(2)]
    return lax.all_gather(pair, "space", axis_index_groups=groups)


def swapped(block, pairs, parts, shift):
    route = []
    for a, b in pairs:
        for m in range(parts):
            n = (m + shift) % parts
            route += [(a * parts + m, b * parts + n), (b * parts + n, a * parts + m)]
    return lax.ppermute(block, ("space", "mp"), route)


def pairs_of(side, start, down, right):
    pairs = []
    for row in range(side):
        for column in range(side):
            place = row * down + column * right
            if place % 2 == start and place + 1 < side:
                here = row * side + column
                pairs.append((here, here + down * side + right))
    return pairs


def neighbour(block, side, down, right):
    route = []
    for row in range(side):
        for column in range(side):
            if 0 <= row + down < side and 0 <= column + right < side:
                route.append(((row + down) * side + column + right, row * side + column))
    return lax.ppermute(block, "space", route)


def in_lanes(columns):
    height = columns[0].shape[0]
    lane = lax.broadcasted_iota(jnp.int32, (height, 128), 1)
    packed = jnp.broadcast_to(columns[-1], (height, 128))
    for k, column in enumerate(columns[:-1]):
        packed = jnp.where(lane == k, column, packed)
    rows = packed.T
    return [rows[k : k + 1] for k in range(len(columns))]


def tile_spec(edge, width):
    return pl.BlockSpec((1, 1, edge, edge, width), lambda i: (i, 0, 0, 0, 0))


def whole_spec(shape):
    return pl.BlockSpec(shape, lambda i: (0,) * len(shape))


def image_spec(rows):
    return pl.BlockSpec((1, rows, LANES), lambda i: (i, 0, 0))


def teacher_kernel(
    edge, place_ref, tokens_ref, corner_ref, heads_ref, logits_ref, row_a, row_b, column_a, column_b, corners_ref, head_ref
):
    patches = edge * edge

    @pl.when(pl.program_id(0) == 0)
    def _():
        pairs = heads_ref.shape[0]
        cut = head_ref.shape[0] // pairs
        for k in range(pairs):
            head_ref[k * cut : (k + 1) * cut, :] = heads_ref[k, :cut, :]
        corners_ref[...] = jnp.dot(corner_ref[...], head_ref[...], preferred_element_type=F32)

    tokens = tokens_ref[0, 0].reshape(patches, tokens_ref.shape[-1])
    logits = jnp.dot(tokens, head_ref[...], preferred_element_type=F32)
    logits_ref[0] = logits
    cube = logits.reshape(edge, edge, LANES)
    row_even, column_even = place_ref[3] == 1, place_ref[4] == 1
    first, last = cube[0], cube[edge - 1]
    row_a[0] = jnp.where(row_even, last, first)
    row_b[0] = jnp.where(row_even, first, last)
    left, right = cube[:, 0, :], cube[:, edge - 1, :]
    column_a[0] = jnp.where(column_even, right, left)
    column_b[0] = jnp.where(column_even, left, right)


def teacher_logits(place, tokens, corner_tokens, heads):
    images, _, edge, _, width = tokens.shape
    corners = corner_tokens.shape[0]
    patches = edge * edge
    border = jax.ShapeDtypeStruct((images, edge, LANES), F32)
    return pl.pallas_call(
        lambda *refs: teacher_kernel(edge, *refs),
        grid=(images,),
        in_specs=[
            pl.BlockSpec(memory_space=pltpu.SMEM),
            tile_spec(edge, width),
            whole_spec(corner_tokens.shape),
            whole_spec(heads.shape),
        ],
        out_specs=[image_spec(patches)] + [image_spec(edge)] * 4 + [whole_spec((corners, LANES))],
        out_shape=[jax.ShapeDtypeStruct((images, patches, LANES), F32)]
        + [border] * 4
        + [jax.ShapeDtypeStruct((corners, LANES), F32)],
        scratch_shapes=[pltpu.VMEM((width, LANES), heads.dtype)],
        compiler_params=pltpu.CompilerParams(vmem_limit_bytes=16 * 2**20),
        cost_estimate=pl.CostEstimate(
            flops=2 * images * patches * width * LANES,
            bytes_accessed=tokens.size * 2 + heads.size * 2 + images * patches * LANES * 4,
            transcendentals=0,
        ),
        name="teacher_logits",
    )(place, tokens, corner_tokens, heads)


def student_kernel(edge, classes, tokens_ref, heads_ref, logits_ref, lse_ref, head_ref):
    @pl.when(pl.program_id(0) == 0)
    def _():
        pairs = heads_ref.shape[0]
        rest = head_ref.shape[0] // pairs
        cut = heads_ref.shape[1] - rest
        for k in range(pairs):
            head_ref[k * rest : (k + 1) * rest, :] = heads_ref[k, cut:, :]

    tokens = tokens_ref[0, 0].reshape(edge * edge, tokens_ref.shape[-1])
    logits = jnp.dot(tokens, head_ref[...], preferred_element_type=F32)
    logits_ref[0] = logits
    logits = logits[:, :classes]
    top = jnp.max(logits, axis=-1, keepdims=True)
    total = jnp.sum(jnp.exp(logits - top), axis=-1, keepdims=True)
    top, total = in_lanes([top, total])
    lse_ref[pl.ds(pl.program_id(0), 1), :] = top + jnp.log(total)


def student_logits(tokens, heads, classes):
    images, _, edge, _, width = tokens.shape
    patches = edge * edge
    return pl.pallas_call(
        lambda *refs: student_kernel(edge, classes, *refs),
        grid=(images,),
        in_specs=[tile_spec(edge, width), whole_spec(heads.shape)],
        out_specs=[image_spec(patches), whole_spec((images, patches))],
        out_shape=[
            jax.ShapeDtypeStruct((images, patches, LANES), F32),
            jax.ShapeDtypeStruct((images, patches), F32),
        ],
        scratch_shapes=[pltpu.VMEM((width, LANES), heads.dtype)],
        compiler_params=pltpu.CompilerParams(vmem_limit_bytes=16 * 2**20),
        cost_estimate=pl.CostEstimate(
            flops=2 * images * patches * width * LANES,
            bytes_accessed=tokens.size * 2 + heads.size * 2 + images * patches * LANES * 4,
            transcendentals=images * patches * LANES,
        ),
        name="student_logits",
    )(tokens, heads)


def stats_kernel(
    edge,
    classes,
    parts,
    images,
    place_ref,
    student_ref,
    lse_ref,
    logits_ref,
    row_a,
    row_b,
    column_a,
    column_b,
    corners_ref,
    out_ref,
):
    image = pl.program_id(0)
    patches = edge * edge
    shape = (edge, edge, LANES)
    row_even, column_even = place_ref[3] == 1, place_ref[4] == 1

    up = jnp.where(row_even, row_b[0], row_a[0])
    down = jnp.where(row_even, row_a[0], row_b[0])
    cube = logits_ref[0].reshape(shape)
    above = jnp.concatenate([up[None], cube[:-1]], axis=0)
    below = jnp.concatenate([cube[1:], down[None]], axis=0)
    columns = above + cube + below
    flat = columns.reshape(patches, LANES)

    y = lax.broadcasted_iota(jnp.int32, (edge, LANES), 0)

    def corner(k):
        return corners_ref[pl.ds(k * images + image, 1), :]

    def side_column(line, top, bottom):
        over = jnp.where(y == 0, top, pltpu.roll(line, 1, 0))
        under = jnp.where(y == edge - 1, bottom, pltpu.roll(line, edge - 1, 0))
        return jnp.broadcast_to((line + over + under)[:, None, :], shape)

    x = lax.broadcasted_iota(jnp.int32, shape, 1)
    to_left = side_column(jnp.where(column_even, column_b[0], column_a[0]), corner(0), corner(2))
    to_right = side_column(jnp.where(column_even, column_a[0], column_b[0]), corner(1), corner(3))
    before = jnp.where(x == 0, to_left, pltpu.roll(flat, 1, 0).reshape(shape))
    after = jnp.where(x == edge - 1, to_right, pltpu.roll(flat, patches - 1, 0).reshape(shape))
    total = columns + before + after

    extent = place_ref[2]
    place_y = place_ref[0] + lax.broadcasted_iota(jnp.int32, (edge, edge, 1), 0)
    place_x = place_ref[1] + lax.broadcasted_iota(jnp.int32, (edge, edge, 1), 1)

    def line(place):
        return 1.0 + (place > 0).astype(F32) + (place < extent - 1).astype(F32)

    share = 1.0 / (line(place_y) * line(place_x))
    smoothed = (total * share).reshape(patches, LANES)[:, :classes]
    student = student_ref[0][:, :classes]

    top_t = jnp.max(smoothed, axis=-1, keepdims=True)
    expo_t = jnp.exp(smoothed - top_t)
    sum_t = jnp.sum(expo_t, axis=-1, keepdims=True)
    gap = jnp.sum(expo_t * (smoothed - student), axis=-1, keepdims=True)
    top_t, sum_t, gap = in_lanes([top_t, sum_t, gap])
    lse_s = lse_ref[pl.ds(image, 1), :]
    for k, stat in enumerate((top_t + jnp.log(sum_t), gap / sum_t, lse_s)):
        for c in range(parts):
            out_ref[c, pl.ds(k * images + image, 1), :] = stat


def patch_stats(place, student, lse_s, logits, borders, corners, classes, parts):
    images, patches, _ = logits.shape
    edge = borders[0].shape[1]
    return pl.pallas_call(
        lambda *refs: stats_kernel(edge, classes, parts, images, *refs),
        grid=(images,),
        in_specs=[
            pl.BlockSpec(memory_space=pltpu.SMEM),
            image_spec(patches),
            whole_spec((images, patches)),
            image_spec(patches),
            *[image_spec(edge)] * 4,
            whole_spec(corners.shape),
        ],
        out_specs=whole_spec((parts, 3 * images, patches)),
        out_shape=jax.ShapeDtypeStruct((parts, 3 * images, patches), F32),
        compiler_params=pltpu.CompilerParams(vmem_limit_bytes=16 * 2**20),
        cost_estimate=pl.CostEstimate(
            flops=30 * images * patches * LANES,
            bytes_accessed=2 * images * patches * LANES * 4,
            transcendentals=images * patches * LANES,
        ),
        name="patch_stats",
    )(place, student, lse_s, logits, *borders, corners)


def divergence_kernel(images, tiles, stats_ref, valid_ref, divergence_ref, totals_ref):
    lse_t = stats_ref[:, :images, :]
    gap = stats_ref[:, images : 2 * images, :]
    lse_s = stats_ref[:, 2 * images :, :]
    top_t = jnp.max(lse_t, axis=0)
    top_s = jnp.max(lse_s, axis=0)
    share = jnp.exp(lse_t - top_t[None])
    sum_t = jnp.sum(share, axis=0)
    sum_s = jnp.sum(jnp.exp(lse_s - top_s[None]), axis=0)
    mean_gap = jnp.sum(share * gap, axis=0) / sum_t
    divergence = mean_gap - top_t - jnp.log(sum_t) + top_s + jnp.log(sum_s)
    divergence_ref[...] = divergence
    weights = valid_ref[...].astype(F32)
    total = jnp.sum(divergence * weights, axis=1, keepdims=True)
    number = jnp.sum(weights, axis=1, keepdims=True)
    shape = (images, 128)
    lane = lax.broadcasted_iota(jnp.int32, shape, 1)
    row = lax.broadcasted_iota(jnp.int32, shape, 0)
    both = jnp.where(lane == row, total, jnp.where(lane == row + images, number, 0.0))
    line = jnp.sum(both, axis=0, keepdims=True)
    totals_ref[...] = jnp.broadcast_to(line[None], totals_ref.shape)


def patch_divergence(stats, valid, tiles):
    images, patches = valid.shape
    whole = pl.BlockSpec(memory_space=pltpu.VMEM)
    return pl.pallas_call(
        lambda *refs: divergence_kernel(images, tiles, *refs),
        in_specs=[whole, whole],
        out_specs=[whole, whole],
        out_shape=[
            jax.ShapeDtypeStruct((images, patches), F32),
            jax.ShapeDtypeStruct((tiles, 1, 128), F32),
        ],
        compiler_params=pltpu.CompilerParams(vmem_limit_bytes=8 * 2**20),
        name="patch_divergence",
    )(stats, valid)


def everywhere_sum(x, tiles, parts):
    groups = []
    for start in range(parts):
        groups.append([t * parts + (start + t % 2 * (parts // 2)) % parts for t in range(tiles)])
    everyone = lax.all_to_all(
        x, ("space", "mp"), split_axis=0, concat_axis=0, tiled=True, axis_index_groups=groups
    )
    return jnp.sum(everyone, axis=(0, 1))


def body(teacher_tokens, student_tokens, teacher_head, student_head, valid):
    tiles = lax.axis_size("space")
    parts = lax.axis_size("mp")
    side = math.isqrt(tiles)
    tile_index = lax.axis_index("space")
    row, column = tile_index // side, tile_index % side
    images, _, edge, _, _ = teacher_tokens.shape
    classes = teacher_head.shape[1]
    flags = valid.reshape(images, edge * edge)
    place = jnp.stack([row * edge, column * edge, side * edge, 1 - row % 2, 1 - column % 2]).astype(jnp.int32)

    heads = gathered_heads(teacher_head, student_head, tiles)
    around = ((-1, -1, -1, -1), (-1, 1, -1, 0), (1, -1, 0, -1), (1, 1, 0, 0))
    corner_tokens = jnp.concatenate(
        [neighbour(teacher_tokens[:, 0, y, x], side, down, right) for down, right, y, x in around]
    )
    logits, row_a, row_b, column_a, column_b, corners = teacher_logits(place, teacher_tokens, corner_tokens, heads)
    borders = [
        swapped(row_a, pairs_of(side, 0, 1, 0), parts, 0),
        swapped(row_b, pairs_of(side, 1, 1, 0), parts, 0),
        swapped(column_a, pairs_of(side, 0, 0, 1), parts, 0),
        swapped(column_b, pairs_of(side, 1, 0, 1), parts, 0),
    ]
    student, lse_s = student_logits(student_tokens, heads, classes)
    stats = patch_stats(place, student, lse_s, logits, borders, corners, classes, parts)
    stats = exchange(stats, "mp")
    divergence, totals = patch_divergence(stats, flags, tiles)
    totals = everywhere_sum(totals, tiles, parts)
    image_loss = totals[:images] / jnp.maximum(totals[images : 2 * images], 1.0)
    return (divergence.reshape(images, 1, edge, edge), image_loss)


def solution(mesh):
    in_specs = (
        P("dp", "space", None, None, None),
        P("dp", "space", None, None, None),
        P(("dp", "space"), "mp"),
        P(("dp", "space"), "mp"),
        P("dp", "space", None, None),
    )
    out_specs = (P("dp", "space", None, None), P("dp"))
    return jax.shard_map(body, mesh=mesh, in_specs=in_specs, out_specs=out_specs, check_vma=False)
```

```python
import math

import jax
import jax.numpy as jnp
from jax import lax
from jax.experimental import pallas as pl
from jax.experimental.pallas import tpu as pltpu
from jax.sharding import PartitionSpec as P

F32 = jnp.float32
LANES = 256


def copies(x, count):
    return jnp.broadcast_to(x, (count, *x.shape))


def exchange(x, axis):
    return lax.all_to_all(x, axis, split_axis=0, concat_axis=0, tiled=True)


def gathered_heads(teacher_head, student_head, tiles):
    cut, classes = teacher_head.shape
    own = jnp.concatenate([teacher_head, student_head])
    own = jnp.pad(own, ((0, 0), (0, LANES - classes)))
    everyone = exchange(copies(own, tiles), "space")
    return everyone[:, :cut].reshape(-1, LANES), everyone[:, cut:].reshape(-1, LANES)


def swapped(block, pairs, parts, shift):
    route = []
    for a, b in pairs:
        for m in range(parts):
            n = (m + shift) % parts
            route += [(a * parts + m, b * parts + n), (b * parts + n, a * parts + m)]
    return lax.ppermute(block, ("space", "mp"), route)


def pairs_of(side, start, down, right):
    pairs = []
    for row in range(side):
        for column in range(side):
            place = row * down + column * right
            if place % 2 == start and place + 1 < side:
                here = row * side + column
                pairs.append((here, here + down * side + right))
    return pairs


def neighbour(block, side, down, right):
    route = []
    for row in range(side):
        for column in range(side):
            if 0 <= row + down < side and 0 <= column + right < side:
                route.append(((row + down) * side + column + right, row * side + column))
    return lax.ppermute(block, "space", route)


def in_lanes(columns):
    height = columns[0].shape[0]
    lane = lax.broadcasted_iota(jnp.int32, (height, 128), 1)
    packed = jnp.broadcast_to(columns[-1], (height, 128))
    for k, column in enumerate(columns[:-1]):
        packed = jnp.where(lane == k, column, packed)
    rows = packed.T
    return [rows[k : k + 1] for k in range(len(columns))]


def whole_spec(shape):
    return pl.BlockSpec(shape, lambda i: (0,) * len(shape))


def image_spec(rows):
    return pl.BlockSpec((1, rows, LANES), lambda i: (i, 0, 0))


def teacher_kernel(
    place_ref,
    source,
    corner_ref,
    head_ref,
    logits_ref,
    row_a,
    row_b,
    column_a,
    column_b,
    corners_ref,
    tokens_ref,
    semaphores,
):
    images, edge, _, width = tokens_ref.shape
    moves = [pltpu.make_async_copy(source.at[i, 0], tokens_ref.at[i], semaphores.at[i]) for i in range(images)]
    for move in moves:
        move.start()
    row_even, column_even = place_ref[3] == 1, place_ref[4] == 1
    corners_ref[...] = jnp.dot(corner_ref[...], head_ref[...], preferred_element_type=F32)
    for i, move in enumerate(moves):
        move.wait()
        tokens = tokens_ref[i].reshape(edge * edge, width)
        logits = jnp.dot(tokens, head_ref[...], preferred_element_type=F32)
        logits_ref[i] = logits
        cube = logits.reshape(edge, edge, LANES)
        first, last = cube[0], cube[edge - 1]
        row_a[i] = jnp.where(row_even, last, first)
        row_b[i] = jnp.where(row_even, first, last)
        left, right = cube[:, 0, :], cube[:, edge - 1, :]
        column_a[i] = jnp.where(column_even, right, left)
        column_b[i] = jnp.where(column_even, left, right)


def teacher_logits(place, tokens, corner_tokens, head):
    images, _, edge, _, width = tokens.shape
    corners = corner_tokens.shape[0]
    patches = edge * edge
    border = jax.ShapeDtypeStruct((images, edge, LANES), F32)
    whole = pl.BlockSpec(memory_space=pltpu.VMEM)
    return pl.pallas_call(
        teacher_kernel,
        in_specs=[
            pl.BlockSpec(memory_space=pltpu.SMEM),
            pl.BlockSpec(memory_space=pltpu.HBM),
            whole,
            whole,
        ],
        out_specs=[whole] * 6,
        out_shape=[jax.ShapeDtypeStruct((images, patches, LANES), F32)]
        + [border] * 4
        + [jax.ShapeDtypeStruct((corners, LANES), F32)],
        scratch_shapes=[pltpu.VMEM((images, edge, edge, width), tokens.dtype), pltpu.SemaphoreType.DMA((images,))],
        compiler_params=pltpu.CompilerParams(vmem_limit_bytes=50 * 2**20),
        cost_estimate=pl.CostEstimate(
            flops=2 * images * patches * width * LANES,
            bytes_accessed=tokens.size * 2 + head.size * 2 + images * patches * LANES * 4,
            transcendentals=0,
        ),
        name="teacher_logits",
    )(place, tokens, corner_tokens, head)


def student_kernel(edge, classes, tokens_ref, head_ref, logits_ref, lse_ref):
    tokens = tokens_ref[pl.program_id(0), 0].reshape(edge * edge, tokens_ref.shape[-1])
    logits = jnp.dot(tokens, head_ref[...], preferred_element_type=F32)
    logits_ref[0] = logits
    logits = logits[:, :classes]
    top = jnp.max(logits, axis=-1, keepdims=True)
    total = jnp.sum(jnp.exp(logits - top), axis=-1, keepdims=True)
    top, total = in_lanes([top, total])
    lse_ref[pl.ds(pl.program_id(0), 1), :] = top + jnp.log(total)


def student_logits(tokens, head, classes):
    images, _, edge, _, width = tokens.shape
    patches = edge * edge
    return pl.pallas_call(
        lambda *refs: student_kernel(edge, classes, *refs),
        grid=(images,),
        in_specs=[pl.BlockSpec(memory_space=pltpu.VMEM), whole_spec(head.shape)],
        out_specs=[image_spec(patches), whole_spec((images, patches))],
        out_shape=[
            jax.ShapeDtypeStruct((images, patches, LANES), F32),
            jax.ShapeDtypeStruct((images, patches), F32),
        ],
        compiler_params=pltpu.CompilerParams(vmem_limit_bytes=16 * 2**20),
        cost_estimate=pl.CostEstimate(
            flops=2 * images * patches * width * LANES,
            bytes_accessed=tokens.size * 2 + head.size * 2 + images * patches * LANES * 4,
            transcendentals=images * patches * LANES,
        ),
        name="student_logits",
    )(tokens, head)


def stats_kernel(
    edge,
    classes,
    parts,
    images,
    place_ref,
    student_ref,
    lse_ref,
    logits_ref,
    row_a,
    row_b,
    column_a,
    column_b,
    corners_ref,
    out_ref,
):
    image = pl.program_id(0)
    patches = edge * edge
    shape = (edge, edge, LANES)
    row_even, column_even = place_ref[3] == 1, place_ref[4] == 1

    up = jnp.where(row_even, row_b[0], row_a[0])
    down = jnp.where(row_even, row_a[0], row_b[0])
    cube = logits_ref[0].reshape(shape)
    above = jnp.concatenate([up[None], cube[:-1]], axis=0)
    below = jnp.concatenate([cube[1:], down[None]], axis=0)
    columns = above + cube + below
    flat = columns.reshape(patches, LANES)

    y = lax.broadcasted_iota(jnp.int32, (edge, LANES), 0)

    def corner(k):
        return corners_ref[pl.ds(k * images + image, 1), :]

    def side_column(line, top, bottom):
        over = jnp.where(y == 0, top, pltpu.roll(line, 1, 0))
        under = jnp.where(y == edge - 1, bottom, pltpu.roll(line, edge - 1, 0))
        return jnp.broadcast_to((line + over + under)[:, None, :], shape)

    x = lax.broadcasted_iota(jnp.int32, shape, 1)
    to_left = side_column(jnp.where(column_even, column_b[0], column_a[0]), corner(0), corner(2))
    to_right = side_column(jnp.where(column_even, column_a[0], column_b[0]), corner(1), corner(3))
    before = jnp.where(x == 0, to_left, pltpu.roll(flat, 1, 0).reshape(shape))
    after = jnp.where(x == edge - 1, to_right, pltpu.roll(flat, patches - 1, 0).reshape(shape))
    total = columns + before + after

    extent = place_ref[2]
    place_y = place_ref[0] + lax.broadcasted_iota(jnp.int32, (edge, edge, 1), 0)
    place_x = place_ref[1] + lax.broadcasted_iota(jnp.int32, (edge, edge, 1), 1)

    def line(place):
        return 1.0 + (place > 0).astype(F32) + (place < extent - 1).astype(F32)

    share = 1.0 / (line(place_y) * line(place_x))
    smoothed = (total * share).reshape(patches, LANES)[:, :classes]
    student = student_ref[0][:, :classes]

    top_t = jnp.max(smoothed, axis=-1, keepdims=True)
    expo_t = jnp.exp(smoothed - top_t)
    sum_t = jnp.sum(expo_t, axis=-1, keepdims=True)
    gap = jnp.sum(expo_t * (smoothed - student), axis=-1, keepdims=True)
    top_t, sum_t, gap = in_lanes([top_t, sum_t, gap])
    lse_s = lse_ref[pl.ds(image, 1), :]
    for k, stat in enumerate((top_t + jnp.log(sum_t), gap / sum_t, lse_s)):
        for c in range(parts):
            out_ref[c, pl.ds(k * images + image, 1), :] = stat


def patch_stats(place, student, lse_s, logits, borders, corners, classes, parts):
    images, patches, _ = logits.shape
    edge = borders[0].shape[1]
    return pl.pallas_call(
        lambda *refs: stats_kernel(edge, classes, parts, images, *refs),
        grid=(images,),
        in_specs=[
            pl.BlockSpec(memory_space=pltpu.SMEM),
            image_spec(patches),
            whole_spec((images, patches)),
            image_spec(patches),
            *[image_spec(edge)] * 4,
            whole_spec(corners.shape),
        ],
        out_specs=whole_spec((parts, 3 * images, patches)),
        out_shape=jax.ShapeDtypeStruct((parts, 3 * images, patches), F32),
        compiler_params=pltpu.CompilerParams(vmem_limit_bytes=16 * 2**20),
        cost_estimate=pl.CostEstimate(
            flops=30 * images * patches * LANES,
            bytes_accessed=2 * images * patches * LANES * 4,
            transcendentals=images * patches * LANES,
        ),
        name="patch_stats",
    )(place, student, lse_s, logits, *borders, corners)


def divergence_kernel(images, tiles, stats_ref, valid_ref, divergence_ref, totals_ref):
    lse_t = stats_ref[:, :images, :]
    gap = stats_ref[:, images : 2 * images, :]
    lse_s = stats_ref[:, 2 * images :, :]
    top_t = jnp.max(lse_t, axis=0)
    top_s = jnp.max(lse_s, axis=0)
    share = jnp.exp(lse_t - top_t[None])
    sum_t = jnp.sum(share, axis=0)
    sum_s = jnp.sum(jnp.exp(lse_s - top_s[None]), axis=0)
    mean_gap = jnp.sum(share * gap, axis=0) / sum_t
    divergence = mean_gap - top_t - jnp.log(sum_t) + top_s + jnp.log(sum_s)
    divergence_ref[...] = divergence
    weights = valid_ref[...].astype(F32)
    total = jnp.sum(divergence * weights, axis=1, keepdims=True)
    number = jnp.sum(weights, axis=1, keepdims=True)
    shape = (images, 128)
    lane = lax.broadcasted_iota(jnp.int32, shape, 1)
    row = lax.broadcasted_iota(jnp.int32, shape, 0)
    both = jnp.where(lane == row, total, jnp.where(lane == row + images, number, 0.0))
    line = jnp.sum(both, axis=0, keepdims=True)
    totals_ref[...] = jnp.broadcast_to(line[None], totals_ref.shape)


def patch_divergence(stats, valid, tiles):
    images, patches = valid.shape
    whole = pl.BlockSpec(memory_space=pltpu.VMEM)
    return pl.pallas_call(
        lambda *refs: divergence_kernel(images, tiles, *refs),
        in_specs=[whole, whole],
        out_specs=[whole, whole],
        out_shape=[
            jax.ShapeDtypeStruct((images, patches), F32),
            jax.ShapeDtypeStruct((tiles, 1, 128), F32),
        ],
        compiler_params=pltpu.CompilerParams(vmem_limit_bytes=8 * 2**20),
        name="patch_divergence",
    )(stats, valid)


def everywhere_sum(x, tiles, parts):
    groups = []
    for start in range(parts):
        groups.append([t * parts + (start + t % 2 * (parts // 2)) % parts for t in range(tiles)])
    everyone = lax.all_to_all(
        x, ("space", "mp"), split_axis=0, concat_axis=0, tiled=True, axis_index_groups=groups
    )
    return jnp.sum(everyone, axis=(0, 1))


def body(teacher_tokens, student_tokens, teacher_head, student_head, valid):
    tiles = lax.axis_size("space")
    parts = lax.axis_size("mp")
    side = math.isqrt(tiles)
    tile_index = lax.axis_index("space")
    row, column = tile_index // side, tile_index % side
    images, _, edge, _, _ = teacher_tokens.shape
    classes = teacher_head.shape[1]
    flags = valid.reshape(images, edge * edge)
    place = jnp.stack([row * edge, column * edge, side * edge, 1 - row % 2, 1 - column % 2]).astype(jnp.int32)

    head_t, head_s = gathered_heads(teacher_head, student_head, tiles)
    around = ((-1, -1, -1, -1), (-1, 1, -1, 0), (1, -1, 0, -1), (1, 1, 0, 0))
    corner_tokens = jnp.concatenate(
        [neighbour(teacher_tokens[:, 0, y, x], side, down, right) for down, right, y, x in around]
    )
    logits, row_a, row_b, column_a, column_b, corners = teacher_logits(
        place, teacher_tokens, corner_tokens, head_t
    )
    column_a = swapped(column_a, pairs_of(side, 0, 0, 1), parts, 0)
    column_b = swapped(column_b, pairs_of(side, 1, 0, 1), parts, 0)
    row_a = swapped(row_a, pairs_of(side, 0, 1, 0), parts, 0)
    row_b = swapped(row_b, pairs_of(side, 1, 1, 0), parts, 0)
    borders = [row_a, row_b, column_a, column_b]
    student, lse_s = student_logits(student_tokens, head_s, classes)
    stats = patch_stats(place, student, lse_s, logits, borders, corners, classes, parts)
    stats = exchange(stats, "mp")
    divergence, totals = patch_divergence(stats, flags, tiles)
    totals = everywhere_sum(totals, tiles, parts)
    image_loss = totals[:images] / jnp.maximum(totals[images : 2 * images], 1.0)
    return (divergence.reshape(images, 1, edge, edge), image_loss)


def solution(mesh):
    in_specs = (
        P("dp", "space", None, None, None),
        P("dp", "space", None, None, None),
        P(("dp", "space"), "mp"),
        P(("dp", "space"), "mp"),
        P("dp", "space", None, None),
    )
    out_specs = (P("dp", "space", None, None), P("dp"))
    return jax.shard_map(body, mesh=mesh, in_specs=in_specs, out_specs=out_specs, check_vma=False)
```

```python
import math

import jax
import jax.numpy as jnp
from jax import lax
from jax.experimental import pallas as pl
from jax.experimental.pallas import tpu as pltpu
from jax.sharding import PartitionSpec as P

F32 = jnp.float32
LANES = 256
BLOCK = 4


def copies(x, count):
    return jnp.broadcast_to(x, (count, *x.shape))


def exchange(x, axis):
    return lax.all_to_all(x, axis, split_axis=0, concat_axis=0, tiled=True)


def padded(head):
    return jnp.pad(head, ((0, 0), (0, LANES - head.shape[1])))


def gathered_heads(teacher_head, student_head, tiles):
    first = exchange(copies(padded(teacher_head), tiles), "space")
    own = padded(student_head)
    other = lax.ppermute(own, "space", [(t, t ^ 1) for t in range(tiles)])
    even = lax.axis_index("space") % 2 == 0
    pair = jnp.concatenate([jnp.where(even, own, other), jnp.where(even, other, own)])
    second, first = lax.optimization_barrier((copies(pair, tiles // 2), first))
    groups = [list(range(z, tiles, 2)) for z in range(2)]
    second = lax.all_to_all(second, "space", split_axis=0, concat_axis=0, tiled=True, axis_index_groups=groups)
    return first.reshape(-1, LANES), second.reshape(-1, LANES)


def swapped(block, pairs, parts, shift):
    route = []
    for a, b in pairs:
        for m in range(parts):
            n = (m + shift) % parts
            route += [(a * parts + m, b * parts + n), (b * parts + n, a * parts + m)]
    return lax.ppermute(block, ("space", "mp"), route)


def pairs_of(side, start, down, right):
    pairs = []
    for row in range(side):
        for column in range(side):
            place = row * down + column * right
            if place % 2 == start and place + 1 < side:
                here = row * side + column
                pairs.append((here, here + down * side + right))
    return pairs


def in_lanes(columns):
    height = columns[0].shape[0]
    lane = lax.broadcasted_iota(jnp.int32, (height, 128), 1)
    packed = jnp.broadcast_to(columns[-1], (height, 128))
    for k, column in enumerate(columns[:-1]):
        packed = jnp.where(lane == k, column, packed)
    rows = packed.T
    return [rows[k : k + 1] for k in range(len(columns))]


def whole_spec(shape):
    return pl.BlockSpec(shape, lambda i: (0,) * len(shape))


def image_spec(rows):
    return pl.BlockSpec((1, rows, LANES), lambda i: (i, 0, 0))


def teacher_kernel(place_ref, tokens_ref, head_ref, logits_ref, row_a, row_b, column_a, column_b):
    edge, width = tokens_ref.shape[2], tokens_ref.shape[-1]
    block, patches, _ = logits_ref.shape
    here = pl.ds(pl.program_id(0) * block, block)
    tokens = tokens_ref[here, 0].reshape(block * patches, width)
    logits = jnp.dot(tokens, head_ref[...], preferred_element_type=F32)
    row_even, column_even = place_ref[3] == 1, place_ref[4] == 1
    for i in range(block):
        image = logits[i * patches : (i + 1) * patches]
        logits_ref[i] = image
        cube = image.reshape(edge, edge, LANES)
        first, last = cube[0], cube[edge - 1]
        row_a[i] = jnp.where(row_even, last, first)
        row_b[i] = jnp.where(row_even, first, last)
        left, right = cube[:, 0, :], cube[:, edge - 1, :]
        column_a[i] = jnp.where(column_even, right, left)
        column_b[i] = jnp.where(column_even, left, right)


def teacher_logits(place, tokens, head):
    images, _, edge, _, width = tokens.shape
    patches = edge * edge
    block = math.gcd(images, BLOCK)
    border = jax.ShapeDtypeStruct((images, edge, LANES), F32)

    def spec(rows):
        return pl.BlockSpec((block, rows, LANES), lambda i: (i, 0, 0))

    return pl.pallas_call(
        teacher_kernel,
        grid=(images // block,),
        in_specs=[
            pl.BlockSpec(memory_space=pltpu.SMEM),
            pl.BlockSpec(memory_space=pltpu.VMEM),
            pl.BlockSpec(memory_space=pltpu.VMEM),
        ],
        out_specs=[spec(patches)] + [spec(edge)] * 4,
        out_shape=[jax.ShapeDtypeStruct((images, patches, LANES), F32)] + [border] * 4,
        compiler_params=pltpu.CompilerParams(vmem_limit_bytes=16 * 2**20),
        cost_estimate=pl.CostEstimate(
            flops=2 * images * patches * width * LANES,
            bytes_accessed=tokens.size * 2 + head.size * 2 + images * patches * LANES * 4,
            transcendentals=0,
        ),
        name="teacher_logits",
    )(place, tokens, head)


def row_kernel(place_ref, row_a, row_b, column_a, column_b, out_a, out_b):
    images, edge, _ = row_a.shape
    row_even, column_even = place_ref[3] == 1, place_ref[4] == 1
    left = jnp.where(column_even, column_b[...], column_a[...])
    right = jnp.where(column_even, column_a[...], column_b[...])
    x = lax.broadcasted_iota(jnp.int32, (edge, LANES), 0)
    for row, out, at_end in ((row_a, out_a, row_even), (row_b, out_b, ~row_even)):
        for i in range(images):
            line = row[i]
            start = jnp.where(at_end, left[i, edge - 1 :], left[i, :1])
            end = jnp.where(at_end, right[i, edge - 1 :], right[i, :1])
            before = jnp.where(x == 0, start, pltpu.roll(line, 1, 0))
            after = jnp.where(x == edge - 1, end, pltpu.roll(line, edge - 1, 0))
            out[i] = line + before + after


def row_sums(place, row_a, row_b, column_a, column_b):
    whole = pl.BlockSpec(memory_space=pltpu.VMEM)
    return pl.pallas_call(
        row_kernel,
        in_specs=[pl.BlockSpec(memory_space=pltpu.SMEM)] + [whole] * 4,
        out_specs=[whole] * 2,
        out_shape=[jax.ShapeDtypeStruct(row_a.shape, F32)] * 2,
        compiler_params=pltpu.CompilerParams(vmem_limit_bytes=4 * 2**20),
        cost_estimate=pl.CostEstimate(flops=10 * row_a.size, bytes_accessed=24 * row_a.size, transcendentals=0),
        name="row_sums",
    )(place, row_a, row_b, column_a, column_b)


def student_kernel(edge, classes, tokens_ref, head_ref, logits_ref, lse_ref):
    tokens = tokens_ref[pl.program_id(0), 0].reshape(edge * edge, tokens_ref.shape[-1])
    logits = jnp.dot(tokens, head_ref[...], preferred_element_type=F32)
    logits_ref[0] = logits
    logits = logits[:, :classes]
    top = jnp.max(logits, axis=-1, keepdims=True)
    total = jnp.sum(jnp.exp(logits - top), axis=-1, keepdims=True)
    top, total = in_lanes([top, total])
    lse_ref[pl.ds(pl.program_id(0), 1), :] = top + jnp.log(total)


def student_logits(tokens, head, classes):
    images, _, edge, _, width = tokens.shape
    patches = edge * edge
    return pl.pallas_call(
        lambda *refs: student_kernel(edge, classes, *refs),
        grid=(images,),
        in_specs=[pl.BlockSpec(memory_space=pltpu.VMEM), whole_spec(head.shape)],
        out_specs=[image_spec(patches), whole_spec((images, patches))],
        out_shape=[
            jax.ShapeDtypeStruct((images, patches, LANES), F32),
            jax.ShapeDtypeStruct((images, patches), F32),
        ],
        compiler_params=pltpu.CompilerParams(vmem_limit_bytes=16 * 2**20),
        cost_estimate=pl.CostEstimate(
            flops=2 * images * patches * width * LANES,
            bytes_accessed=tokens.size * 2 + head.size * 2 + images * patches * LANES * 4,
            transcendentals=images * patches * LANES,
        ),
        name="student_logits",
    )(tokens, head)


def stats_kernel(
    edge,
    classes,
    parts,
    images,
    place_ref,
    student_ref,
    lse_ref,
    logits_ref,
    row_a,
    row_b,
    column_a,
    column_b,
    out_ref,
):
    image = pl.program_id(0)
    patches = edge * edge
    shape = (edge, edge, LANES)
    row_even, column_even = place_ref[3] == 1, place_ref[4] == 1

    flat = logits_ref[0]
    cube = flat.reshape(shape)
    x = lax.broadcasted_iota(jnp.int32, shape, 1)
    to_left = jnp.broadcast_to(jnp.where(column_even, column_b[0], column_a[0])[:, None, :], shape)
    to_right = jnp.broadcast_to(jnp.where(column_even, column_a[0], column_b[0])[:, None, :], shape)
    before = jnp.where(x == 0, to_left, pltpu.roll(flat, 1, 0).reshape(shape))
    after = jnp.where(x == edge - 1, to_right, pltpu.roll(flat, patches - 1, 0).reshape(shape))
    rows = cube + before + after
    up = jnp.where(row_even, row_b[0], row_a[0])
    down = jnp.where(row_even, row_a[0], row_b[0])
    above = jnp.concatenate([up[None], rows[:-1]], axis=0)
    below = jnp.concatenate([rows[1:], down[None]], axis=0)
    total = rows + above + below

    extent = place_ref[2]
    place_y = place_ref[0] + lax.broadcasted_iota(jnp.int32, (edge, edge, 1), 0)
    place_x = place_ref[1] + lax.broadcasted_iota(jnp.int32, (edge, edge, 1), 1)

    def line(place):
        return 1.0 + (place > 0).astype(F32) + (place < extent - 1).astype(F32)

    share = 1.0 / (line(place_y) * line(place_x))
    smoothed = (total * share).reshape(patches, LANES)[:, :classes]
    student = student_ref[0][:, :classes]

    top_t = jnp.max(smoothed, axis=-1, keepdims=True)
    expo_t = jnp.exp(smoothed - top_t)
    sum_t = jnp.sum(expo_t, axis=-1, keepdims=True)
    gap = jnp.sum(expo_t * (smoothed - student), axis=-1, keepdims=True)
    top_t, sum_t, gap = in_lanes([top_t, sum_t, gap])
    lse_s = lse_ref[pl.ds(image, 1), :]
    for k, stat in enumerate((top_t + jnp.log(sum_t), gap / sum_t, lse_s)):
        for c in range(parts):
            out_ref[c, pl.ds(k * images + image, 1), :] = stat


def patch_stats(place, student, lse_s, logits, borders, classes, parts):
    images, patches, _ = logits.shape
    edge = borders[0].shape[1]
    return pl.pallas_call(
        lambda *refs: stats_kernel(edge, classes, parts, images, *refs),
        grid=(images,),
        in_specs=[
            pl.BlockSpec(memory_space=pltpu.SMEM),
            image_spec(patches),
            whole_spec((images, patches)),
            image_spec(patches),
            *[image_spec(edge)] * 4,
        ],
        out_specs=whole_spec((parts, 3 * images, patches)),
        out_shape=jax.ShapeDtypeStruct((parts, 3 * images, patches), F32),
        compiler_params=pltpu.CompilerParams(vmem_limit_bytes=16 * 2**20),
        cost_estimate=pl.CostEstimate(
            flops=30 * images * patches * LANES,
            bytes_accessed=2 * images * patches * LANES * 4,
            transcendentals=images * patches * LANES,
        ),
        name="patch_stats",
    )(place, student, lse_s, logits, *borders)


def divergence_kernel(images, tiles, stats_ref, valid_ref, divergence_ref, totals_ref):
    lse_t = stats_ref[:, :images, :]
    gap = stats_ref[:, images : 2 * images, :]
    lse_s = stats_ref[:, 2 * images :, :]
    top_t = jnp.max(lse_t, axis=0)
    top_s = jnp.max(lse_s, axis=0)
    share = jnp.exp(lse_t - top_t[None])
    sum_t = jnp.sum(share, axis=0)
    sum_s = jnp.sum(jnp.exp(lse_s - top_s[None]), axis=0)
    mean_gap = jnp.sum(share * gap, axis=0) / sum_t
    divergence = mean_gap - top_t - jnp.log(sum_t) + top_s + jnp.log(sum_s)
    divergence_ref[...] = divergence
    weights = valid_ref[...].astype(F32)
    total = jnp.sum(divergence * weights, axis=1, keepdims=True)
    number = jnp.sum(weights, axis=1, keepdims=True)
    shape = (images, 128)
    lane = lax.broadcasted_iota(jnp.int32, shape, 1)
    row = lax.broadcasted_iota(jnp.int32, shape, 0)
    both = jnp.where(lane == row, total, jnp.where(lane == row + images, number, 0.0))
    line = jnp.sum(both, axis=0, keepdims=True)
    totals_ref[...] = jnp.broadcast_to(line[None], totals_ref.shape)


def patch_divergence(stats, valid, tiles):
    images, patches = valid.shape
    whole = pl.BlockSpec(memory_space=pltpu.VMEM)
    return pl.pallas_call(
        lambda *refs: divergence_kernel(images, tiles, *refs),
        in_specs=[whole, whole],
        out_specs=[whole, whole],
        out_shape=[
            jax.ShapeDtypeStruct((images, patches), F32),
            jax.ShapeDtypeStruct((tiles, 1, 128), F32),
        ],
        compiler_params=pltpu.CompilerParams(vmem_limit_bytes=8 * 2**20),
        name="patch_divergence",
    )(stats, valid)


def everywhere_sum(x, tiles, parts):
    groups = []
    for start in range(parts):
        groups.append([t * parts + (start + t % 2 * (parts // 2)) % parts for t in range(tiles)])
    everyone = lax.all_to_all(
        x, ("space", "mp"), split_axis=0, concat_axis=0, tiled=True, axis_index_groups=groups
    )
    return jnp.sum(everyone, axis=(0, 1))


def body(teacher_tokens, student_tokens, teacher_head, student_head, valid):
    tiles = lax.axis_size("space")
    parts = lax.axis_size("mp")
    side = math.isqrt(tiles)
    tile_index = lax.axis_index("space")
    row, column = tile_index // side, tile_index % side
    images, _, edge, _, _ = teacher_tokens.shape
    classes = teacher_head.shape[1]
    flags = valid.reshape(images, edge * edge)
    place = jnp.stack([row * edge, column * edge, side * edge, 1 - row % 2, 1 - column % 2]).astype(jnp.int32)

    head_t, head_s = gathered_heads(teacher_head, student_head, tiles)
    logits, row_a, row_b, column_a, column_b = teacher_logits(place, teacher_tokens, head_t)
    column_a = swapped(column_a, pairs_of(side, 0, 0, 1), parts, 0)
    column_b = swapped(column_b, pairs_of(side, 1, 0, 1), parts, 0)
    row_a, row_b = row_sums(place, row_a, row_b, column_a, column_b)
    row_a = swapped(row_a, pairs_of(side, 0, 1, 0), parts, 0)
    row_b = swapped(row_b, pairs_of(side, 1, 1, 0), parts, 0)
    student, lse_s = student_logits(student_tokens, head_s, classes)
    stats = patch_stats(place, student, lse_s, logits, [row_a, row_b, column_a, column_b], classes, parts)
    stats = exchange(stats, "mp")
    divergence, totals = patch_divergence(stats, flags, tiles)
    totals = everywhere_sum(totals, tiles, parts)
    image_loss = totals[:images] / jnp.maximum(totals[images : 2 * images], 1.0)
    return (divergence.reshape(images, 1, edge, edge), image_loss)


def solution(mesh):
    in_specs = (
        P("dp", "space", None, None, None),
        P("dp", "space", None, None, None),
        P(("dp", "space"), "mp"),
        P(("dp", "space"), "mp"),
        P("dp", "space", None, None),
    )
    out_specs = (P("dp", "space", None, None), P("dp"))
    return jax.shard_map(body, mesh=mesh, in_specs=in_specs, out_specs=out_specs, check_vma=False)
```

```python
import math

import jax
import jax.numpy as jnp
from jax import lax
from jax.experimental import pallas as pl
from jax.experimental.pallas import tpu as pltpu
from jax.sharding import PartitionSpec as P

F32 = jnp.float32
LANES = 256
BLOCK = 4


def copies(x, count):
    return jnp.broadcast_to(x, (count, *x.shape))


def exchange(x, axis):
    return lax.all_to_all(x, axis, split_axis=0, concat_axis=0, tiled=True)


def padded(head):
    return jnp.pad(head, ((0, 0), (0, LANES - head.shape[1])))


def gathered_heads(teacher_head, student_head, tiles):
    cut = teacher_head.shape[0]
    own = padded(jnp.concatenate([teacher_head, student_head]))
    other = lax.ppermute(own, "space", [(t, t ^ 1) for t in range(tiles)])
    is_even = lax.axis_index("space") % 2 == 0
    even, odd = jnp.where(is_even, own, other), jnp.where(is_even, other, own)
    groups = [list(range(z, tiles, 2)) for z in range(2)]

    def along_y(pair):
        return lax.all_to_all(pair, "space", split_axis=0, concat_axis=0, tiled=True, axis_index_groups=groups)

    first = along_y(copies(jnp.concatenate([even[:cut], odd[:cut]]), tiles // 2))
    second = copies(jnp.concatenate([even[cut:], odd[cut:]]), tiles // 2)
    second, first = lax.optimization_barrier((second, first))
    second = along_y(second)
    return first.reshape(-1, LANES), second.reshape(-1, LANES)


def swapped(block, pairs, parts, shift):
    route = []
    for a, b in pairs:
        for m in range(parts):
            n = (m + shift) % parts
            route += [(a * parts + m, b * parts + n), (b * parts + n, a * parts + m)]
    return lax.ppermute(block, ("space", "mp"), route)


def pairs_of(side, start, down, right):
    pairs = []
    for row in range(side):
        for column in range(side):
            place = row * down + column * right
            if place % 2 == start and place + 1 < side:
                here = row * side + column
                pairs.append((here, here + down * side + right))
    return pairs


def in_lanes(columns):
    height = columns[0].shape[0]
    lane = lax.broadcasted_iota(jnp.int32, (height, 128), 1)
    packed = jnp.broadcast_to(columns[-1], (height, 128))
    for k, column in enumerate(columns[:-1]):
        packed = jnp.where(lane == k, column, packed)
    rows = packed.T
    return [rows[k : k + 1] for k in range(len(columns))]


def whole_spec(shape):
    return pl.BlockSpec(shape, lambda i: (0,) * len(shape))


def image_spec(rows):
    return pl.BlockSpec((1, rows, LANES), lambda i: (i, 0, 0))


def teacher_kernel(place_ref, tokens_ref, head_ref, logits_ref, row_a, row_b, column_a, column_b):
    edge, width = tokens_ref.shape[2], tokens_ref.shape[-1]
    block, patches, _ = logits_ref.shape
    here = pl.ds(pl.program_id(0) * block, block)
    tokens = tokens_ref[here, 0].reshape(block * patches, width)
    logits = jnp.dot(tokens, head_ref[...], preferred_element_type=F32)
    row_even, column_even = place_ref[3] == 1, place_ref[4] == 1
    for i in range(block):
        image = logits[i * patches : (i + 1) * patches]
        logits_ref[i] = image
        cube = image.reshape(edge, edge, LANES)
        first, last = cube[0], cube[edge - 1]
        row_a[i] = jnp.where(row_even, last, first)
        row_b[i] = jnp.where(row_even, first, last)
        left, right = cube[:, 0, :], cube[:, edge - 1, :]
        column_a[i] = jnp.where(column_even, right, left)
        column_b[i] = jnp.where(column_even, left, right)


def teacher_logits(place, tokens, head):
    images, _, edge, _, width = tokens.shape
    patches = edge * edge
    block = math.gcd(images, BLOCK)
    border = jax.ShapeDtypeStruct((images, edge, LANES), F32)

    def spec(rows):
        return pl.BlockSpec((block, rows, LANES), lambda i: (i, 0, 0))

    return pl.pallas_call(
        teacher_kernel,
        grid=(images // block,),
        in_specs=[
            pl.BlockSpec(memory_space=pltpu.SMEM),
            pl.BlockSpec(memory_space=pltpu.VMEM),
            pl.BlockSpec(memory_space=pltpu.VMEM),
        ],
        out_specs=[spec(patches)] + [spec(edge)] * 4,
        out_shape=[jax.ShapeDtypeStruct((images, patches, LANES), F32)] + [border] * 4,
        compiler_params=pltpu.CompilerParams(vmem_limit_bytes=16 * 2**20),
        cost_estimate=pl.CostEstimate(
            flops=2 * images * patches * width * LANES,
            bytes_accessed=tokens.size * 2 + head.size * 2 + images * patches * LANES * 4,
            transcendentals=0,
        ),
        name="teacher_logits",
    )(place, tokens, head)


def row_kernel(place_ref, row_a, row_b, column_a, column_b, out_a, out_b):
    images, edge, _ = row_a.shape
    row_even, column_even = place_ref[3] == 1, place_ref[4] == 1
    left = jnp.where(column_even, column_b[...], column_a[...])
    right = jnp.where(column_even, column_a[...], column_b[...])
    x = lax.broadcasted_iota(jnp.int32, (edge, LANES), 0)
    for row, out, at_end in ((row_a, out_a, row_even), (row_b, out_b, ~row_even)):
        for i in range(images):
            line = row[i]
            start = jnp.where(at_end, left[i, edge - 1 :], left[i, :1])
            end = jnp.where(at_end, right[i, edge - 1 :], right[i, :1])
            before = jnp.where(x == 0, start, pltpu.roll(line, 1, 0))
            after = jnp.where(x == edge - 1, end, pltpu.roll(line, edge - 1, 0))
            out[i] = line + before + after


def row_sums(place, row_a, row_b, column_a, column_b):
    whole = pl.BlockSpec(memory_space=pltpu.VMEM)
    return pl.pallas_call(
        row_kernel,
        in_specs=[pl.BlockSpec(memory_space=pltpu.SMEM)] + [whole] * 4,
        out_specs=[whole] * 2,
        out_shape=[jax.ShapeDtypeStruct(row_a.shape, F32)] * 2,
        compiler_params=pltpu.CompilerParams(vmem_limit_bytes=4 * 2**20),
        cost_estimate=pl.CostEstimate(flops=10 * row_a.size, bytes_accessed=24 * row_a.size, transcendentals=0),
        name="row_sums",
    )(place, row_a, row_b, column_a, column_b)


def student_kernel(edge, classes, tokens_ref, head_ref, logits_ref, lse_ref):
    block, patches, _ = logits_ref.shape
    start = pl.program_id(0) * block
    tokens = tokens_ref[pl.ds(start, block), 0].reshape(block * patches, tokens_ref.shape[-1])
    logits = jnp.dot(tokens, head_ref[...], preferred_element_type=F32)
    for i in range(block):
        image = logits[i * patches : (i + 1) * patches]
        logits_ref[i] = image
        image = image[:, :classes]
        top = jnp.max(image, axis=-1, keepdims=True)
        total = jnp.sum(jnp.exp(image - top), axis=-1, keepdims=True)
        top, total = in_lanes([top, total])
        lse_ref[pl.ds(start + i, 1), :] = top + jnp.log(total)


def student_logits(tokens, head, classes):
    images, _, edge, _, width = tokens.shape
    patches = edge * edge
    block = math.gcd(images, BLOCK)
    return pl.pallas_call(
        lambda *refs: student_kernel(edge, classes, *refs),
        grid=(images // block,),
        in_specs=[pl.BlockSpec(memory_space=pltpu.VMEM), pl.BlockSpec(memory_space=pltpu.VMEM)],
        out_specs=[pl.BlockSpec((block, patches, LANES), lambda i: (i, 0, 0)), whole_spec((images, patches))],
        out_shape=[
            jax.ShapeDtypeStruct((images, patches, LANES), F32),
            jax.ShapeDtypeStruct((images, patches), F32),
        ],
        compiler_params=pltpu.CompilerParams(vmem_limit_bytes=16 * 2**20),
        cost_estimate=pl.CostEstimate(
            flops=2 * images * patches * width * LANES,
            bytes_accessed=tokens.size * 2 + head.size * 2 + images * patches * LANES * 4,
            transcendentals=images * patches * LANES,
        ),
        name="student_logits",
    )(tokens, head)


def stats_kernel(
    edge,
    classes,
    parts,
    images,
    place_ref,
    student_ref,
    lse_ref,
    logits_ref,
    row_a,
    row_b,
    column_a,
    column_b,
    out_ref,
):
    image = pl.program_id(0)
    patches = edge * edge
    shape = (edge, edge, LANES)
    row_even, column_even = place_ref[3] == 1, place_ref[4] == 1

    flat = logits_ref[0]
    cube = flat.reshape(shape)
    x = lax.broadcasted_iota(jnp.int32, shape, 1)
    to_left = jnp.broadcast_to(jnp.where(column_even, column_b[0], column_a[0])[:, None, :], shape)
    to_right = jnp.broadcast_to(jnp.where(column_even, column_a[0], column_b[0])[:, None, :], shape)
    before = jnp.where(x == 0, to_left, pltpu.roll(flat, 1, 0).reshape(shape))
    after = jnp.where(x == edge - 1, to_right, pltpu.roll(flat, patches - 1, 0).reshape(shape))
    rows = cube + before + after
    up = jnp.where(row_even, row_b[0], row_a[0])
    down = jnp.where(row_even, row_a[0], row_b[0])
    above = jnp.concatenate([up[None], rows[:-1]], axis=0)
    below = jnp.concatenate([rows[1:], down[None]], axis=0)
    total = rows + above + below

    extent = place_ref[2]
    place_y = place_ref[0] + lax.broadcasted_iota(jnp.int32, (edge, edge, 1), 0)
    place_x = place_ref[1] + lax.broadcasted_iota(jnp.int32, (edge, edge, 1), 1)

    def line(place):
        return 1.0 + (place > 0).astype(F32) + (place < extent - 1).astype(F32)

    share = 1.0 / (line(place_y) * line(place_x))
    smoothed = (total * share).reshape(patches, LANES)[:, :classes]
    student = student_ref[0][:, :classes]

    top_t = jnp.max(smoothed, axis=-1, keepdims=True)
    expo_t = jnp.exp(smoothed - top_t)
    sum_t = jnp.sum(expo_t, axis=-1, keepdims=True)
    gap = jnp.sum(expo_t * (smoothed - student), axis=-1, keepdims=True)
    top_t, sum_t, gap = in_lanes([top_t, sum_t, gap])
    lse_s = lse_ref[pl.ds(image, 1), :]
    for k, stat in enumerate((top_t + jnp.log(sum_t), gap / sum_t, lse_s)):
        for c in range(parts):
            out_ref[c, pl.ds(k * images + image, 1), :] = stat


def patch_stats(place, student, lse_s, logits, borders, classes, parts):
    images, patches, _ = logits.shape
    edge = borders[0].shape[1]
    return pl.pallas_call(
        lambda *refs: stats_kernel(edge, classes, parts, images, *refs),
        grid=(images,),
        in_specs=[
            pl.BlockSpec(memory_space=pltpu.SMEM),
            image_spec(patches),
            whole_spec((images, patches)),
            image_spec(patches),
            *[image_spec(edge)] * 4,
        ],
        out_specs=whole_spec((parts, 3 * images, patches)),
        out_shape=jax.ShapeDtypeStruct((parts, 3 * images, patches), F32),
        compiler_params=pltpu.CompilerParams(vmem_limit_bytes=16 * 2**20),
        cost_estimate=pl.CostEstimate(
            flops=30 * images * patches * LANES,
            bytes_accessed=2 * images * patches * LANES * 4,
            transcendentals=images * patches * LANES,
        ),
        name="patch_stats",
    )(place, student, lse_s, logits, *borders)


def divergence_kernel(images, tiles, stats_ref, valid_ref, divergence_ref, totals_ref):
    lse_t = stats_ref[:, :images, :]
    gap = stats_ref[:, images : 2 * images, :]
    lse_s = stats_ref[:, 2 * images :, :]
    top_t = jnp.max(lse_t, axis=0)
    top_s = jnp.max(lse_s, axis=0)
    share = jnp.exp(lse_t - top_t[None])
    sum_t = jnp.sum(share, axis=0)
    sum_s = jnp.sum(jnp.exp(lse_s - top_s[None]), axis=0)
    mean_gap = jnp.sum(share * gap, axis=0) / sum_t
    divergence = mean_gap - top_t - jnp.log(sum_t) + top_s + jnp.log(sum_s)
    divergence_ref[...] = divergence
    weights = valid_ref[...].astype(F32)
    total = jnp.sum(divergence * weights, axis=1, keepdims=True)
    number = jnp.sum(weights, axis=1, keepdims=True)
    shape = (images, 128)
    lane = lax.broadcasted_iota(jnp.int32, shape, 1)
    row = lax.broadcasted_iota(jnp.int32, shape, 0)
    both = jnp.where(lane == row, total, jnp.where(lane == row + images, number, 0.0))
    line = jnp.sum(both, axis=0, keepdims=True)
    totals_ref[...] = jnp.broadcast_to(line[None], totals_ref.shape)


def patch_divergence(stats, valid, tiles):
    images, patches = valid.shape
    whole = pl.BlockSpec(memory_space=pltpu.VMEM)
    return pl.pallas_call(
        lambda *refs: divergence_kernel(images, tiles, *refs),
        in_specs=[whole, whole],
        out_specs=[whole, whole],
        out_shape=[
            jax.ShapeDtypeStruct((images, patches), F32),
            jax.ShapeDtypeStruct((tiles, 1, 128), F32),
        ],
        compiler_params=pltpu.CompilerParams(vmem_limit_bytes=8 * 2**20),
        name="patch_divergence",
    )(stats, valid)


def everywhere_sum(x, tiles, parts):
    groups = []
    for start in range(parts):
        groups.append([t * parts + (start + t % 2 * (parts // 2)) % parts for t in range(tiles)])
    everyone = lax.all_to_all(
        x, ("space", "mp"), split_axis=0, concat_axis=0, tiled=True, axis_index_groups=groups
    )
    return jnp.sum(everyone, axis=(0, 1))


def body(teacher_tokens, student_tokens, teacher_head, student_head, valid):
    tiles = lax.axis_size("space")
    parts = lax.axis_size("mp")
    side = math.isqrt(tiles)
    tile_index = lax.axis_index("space")
    row, column = tile_index // side, tile_index % side
    images, _, edge, _, _ = teacher_tokens.shape
    classes = teacher_head.shape[1]
    flags = valid.reshape(images, edge * edge)
    place = jnp.stack([row * edge, column * edge, side * edge, 1 - row % 2, 1 - column % 2]).astype(jnp.int32)

    head_t, head_s = gathered_heads(teacher_head, student_head, tiles)
    logits, row_a, row_b, column_a, column_b = teacher_logits(place, teacher_tokens, head_t)
    column_a = swapped(column_a, pairs_of(side, 0, 0, 1), parts, 0)
    column_b = swapped(column_b, pairs_of(side, 1, 0, 1), parts, 0)
    row_a, row_b = row_sums(place, row_a, row_b, column_a, column_b)
    row_a = swapped(row_a, pairs_of(side, 0, 1, 0), parts, 0)
    row_b = swapped(row_b, pairs_of(side, 1, 1, 0), parts, 0)
    student, lse_s = student_logits(student_tokens, head_s, classes)
    stats = patch_stats(place, student, lse_s, logits, [row_a, row_b, column_a, column_b], classes, parts)
    stats = exchange(stats, "mp")
    divergence, totals = patch_divergence(stats, flags, tiles)
    totals = everywhere_sum(totals, tiles, parts)
    image_loss = totals[:images] / jnp.maximum(totals[images : 2 * images], 1.0)
    return (divergence.reshape(images, 1, edge, edge), image_loss)


def solution(mesh):
    in_specs = (
        P("dp", "space", None, None, None),
        P("dp", "space", None, None, None),
        P(("dp", "space"), "mp"),
        P(("dp", "space"), "mp"),
        P("dp", "space", None, None),
    )
    out_specs = (P("dp", "space", None, None), P("dp"))
    return jax.shard_map(body, mesh=mesh, in_specs=in_specs, out_specs=out_specs, check_vma=False)
```

```python
import math

import jax
import jax.numpy as jnp
from jax import lax
from jax.experimental import pallas as pl
from jax.experimental.pallas import tpu as pltpu
from jax.sharding import PartitionSpec as P

F32 = jnp.float32
LANES = 256
BLOCK = 4


def copies(x, count):
    return jnp.broadcast_to(x, (count, *x.shape))


def exchange(x, axis):
    return lax.all_to_all(x, axis, split_axis=0, concat_axis=0, tiled=True)


def padded(head):
    return jnp.pad(head, ((0, 0), (0, LANES - head.shape[1])))


def gathered_heads(teacher_head, student_head, tiles):
    cut = teacher_head.shape[0]
    own = padded(jnp.concatenate([teacher_head, student_head]))
    other = lax.ppermute(own, "space", [(t, t ^ 1) for t in range(tiles)])
    is_even = lax.axis_index("space") % 2 == 0
    even, odd = jnp.where(is_even, own, other), jnp.where(is_even, other, own)
    groups = [list(range(z, tiles, 2)) for z in range(2)]

    def along_y(pair):
        return lax.all_to_all(pair, "space", split_axis=0, concat_axis=0, tiled=True, axis_index_groups=groups)

    first = along_y(copies(jnp.concatenate([even[:cut], odd[:cut]]), tiles // 2))
    second = copies(jnp.concatenate([even[cut:], odd[cut:]]), tiles // 2)
    second, first = lax.optimization_barrier((second, first))
    second = along_y(second)
    return first.reshape(-1, LANES), second.reshape(-1, LANES)


def swapped(block, pairs, parts, shift):
    route = []
    for a, b in pairs:
        for m in range(parts):
            n = (m + shift) % parts
            route += [(a * parts + m, b * parts + n), (b * parts + n, a * parts + m)]
    return lax.ppermute(block, ("space", "mp"), route)


def pairs_of(side, start, down, right):
    pairs = []
    for row in range(side):
        for column in range(side):
            place = row * down + column * right
            if place % 2 == start and place + 1 < side:
                here = row * side + column
                pairs.append((here, here + down * side + right))
    return pairs


def in_lanes(columns):
    height = columns[0].shape[0]
    lane = lax.broadcasted_iota(jnp.int32, (height, 128), 1)
    packed = jnp.broadcast_to(columns[-1], (height, 128))
    for k, column in enumerate(columns[:-1]):
        packed = jnp.where(lane == k, column, packed)
    rows = packed.T
    return [rows[k : k + 1] for k in range(len(columns))]


def teacher_kernel(block, place_ref, tokens_ref, head_ref, logits_ref, row_a, row_b, column_a, column_b):
    edge, width = tokens_ref.shape[2], tokens_ref.shape[-1]
    images, patches, _ = logits_ref.shape
    row_even, column_even = place_ref[3] == 1, place_ref[4] == 1
    for start in range(0, images, block):
        tokens = tokens_ref[start : start + block, 0].reshape(block * patches, width)
        logits = jnp.dot(tokens, head_ref[...], preferred_element_type=F32)
        for i in range(block):
            image = logits[i * patches : (i + 1) * patches]
            logits_ref[start + i] = image
            cube = image.reshape(edge, edge, LANES)
            first, last = cube[0], cube[edge - 1]
            row_a[start + i] = jnp.where(row_even, last, first)
            row_b[start + i] = jnp.where(row_even, first, last)
            left, right = cube[:, 0, :], cube[:, edge - 1, :]
            column_a[start + i] = jnp.where(column_even, right, left)
            column_b[start + i] = jnp.where(column_even, left, right)


def teacher_logits(place, tokens, head):
    images, _, edge, _, width = tokens.shape
    patches = edge * edge
    border = jax.ShapeDtypeStruct((images, edge, LANES), F32)
    whole = pl.BlockSpec(memory_space=pltpu.VMEM)
    return pl.pallas_call(
        lambda *refs: teacher_kernel(math.gcd(images, BLOCK), *refs),
        in_specs=[pl.BlockSpec(memory_space=pltpu.SMEM), whole, whole],
        out_specs=[whole] * 5,
        out_shape=[jax.ShapeDtypeStruct((images, patches, LANES), F32)] + [border] * 4,
        compiler_params=pltpu.CompilerParams(vmem_limit_bytes=16 * 2**20),
        cost_estimate=pl.CostEstimate(
            flops=2 * images * patches * width * LANES,
            bytes_accessed=tokens.size * 2 + head.size * 2 + images * patches * LANES * 4,
            transcendentals=0,
        ),
        name="teacher_logits",
    )(place, tokens, head)


def row_kernel(place_ref, row_a, row_b, column_a, column_b, out_a, out_b):
    images, edge, _ = row_a.shape
    row_even, column_even = place_ref[3] == 1, place_ref[4] == 1
    left = jnp.where(column_even, column_b[...], column_a[...])
    right = jnp.where(column_even, column_a[...], column_b[...])
    x = lax.broadcasted_iota(jnp.int32, (edge, LANES), 0)
    for row, out, at_end in ((row_a, out_a, row_even), (row_b, out_b, ~row_even)):
        for i in range(images):
            line = row[i]
            start = jnp.where(at_end, left[i, edge - 1 :], left[i, :1])
            end = jnp.where(at_end, right[i, edge - 1 :], right[i, :1])
            before = jnp.where(x == 0, start, pltpu.roll(line, 1, 0))
            after = jnp.where(x == edge - 1, end, pltpu.roll(line, edge - 1, 0))
            out[i] = line + before + after


def row_sums(place, row_a, row_b, column_a, column_b):
    whole = pl.BlockSpec(memory_space=pltpu.VMEM)
    return pl.pallas_call(
        row_kernel,
        in_specs=[pl.BlockSpec(memory_space=pltpu.SMEM)] + [whole] * 4,
        out_specs=[whole] * 2,
        out_shape=[jax.ShapeDtypeStruct(row_a.shape, F32)] * 2,
        compiler_params=pltpu.CompilerParams(vmem_limit_bytes=4 * 2**20),
        cost_estimate=pl.CostEstimate(flops=10 * row_a.size, bytes_accessed=24 * row_a.size, transcendentals=0),
        name="row_sums",
    )(place, row_a, row_b, column_a, column_b)


def student_kernel(block, classes, tokens_ref, head_ref, logits_ref, lse_ref):
    images, patches, _ = logits_ref.shape
    for start in range(0, images, block):
        tokens = tokens_ref[start : start + block, 0].reshape(block * patches, tokens_ref.shape[-1])
        logits = jnp.dot(tokens, head_ref[...], preferred_element_type=F32)
        for i in range(block):
            image = logits[i * patches : (i + 1) * patches]
            logits_ref[start + i] = image
            image = image[:, :classes]
            top = jnp.max(image, axis=-1, keepdims=True)
            total = jnp.sum(jnp.exp(image - top), axis=-1, keepdims=True)
            top, total = in_lanes([top, total])
            lse_ref[start + i : start + i + 1, :] = top + jnp.log(total)


def student_logits(tokens, head, classes):
    images, _, edge, _, width = tokens.shape
    patches = edge * edge
    whole = pl.BlockSpec(memory_space=pltpu.VMEM)
    return pl.pallas_call(
        lambda *refs: student_kernel(math.gcd(images, BLOCK), classes, *refs),
        in_specs=[whole, whole],
        out_specs=[whole, whole],
        out_shape=[
            jax.ShapeDtypeStruct((images, patches, LANES), F32),
            jax.ShapeDtypeStruct((images, patches), F32),
        ],
        compiler_params=pltpu.CompilerParams(vmem_limit_bytes=16 * 2**20),
        cost_estimate=pl.CostEstimate(
            flops=2 * images * patches * width * LANES,
            bytes_accessed=tokens.size * 2 + head.size * 2 + images * patches * LANES * 4,
            transcendentals=images * patches * LANES,
        ),
        name="student_logits",
    )(tokens, head)


def stats_kernel(
    edge,
    classes,
    parts,
    images,
    place_ref,
    student_ref,
    lse_ref,
    logits_ref,
    row_a,
    row_b,
    column_a,
    column_b,
    out_ref,
):
    image = pl.program_id(0)
    patches = edge * edge
    shape = (edge, edge, LANES)
    row_even, column_even = place_ref[3] == 1, place_ref[4] == 1

    flat = logits_ref[image]
    cube = flat.reshape(shape)
    x = lax.broadcasted_iota(jnp.int32, shape, 1)
    to_left = jnp.broadcast_to(jnp.where(column_even, column_b[image], column_a[image])[:, None, :], shape)
    to_right = jnp.broadcast_to(jnp.where(column_even, column_a[image], column_b[image])[:, None, :], shape)
    before = jnp.where(x == 0, to_left, pltpu.roll(flat, 1, 0).reshape(shape))
    after = jnp.where(x == edge - 1, to_right, pltpu.roll(flat, patches - 1, 0).reshape(shape))
    rows = cube + before + after
    up = jnp.where(row_even, row_b[image], row_a[image])
    down = jnp.where(row_even, row_a[image], row_b[image])
    above = jnp.concatenate([up[None], rows[:-1]], axis=0)
    below = jnp.concatenate([rows[1:], down[None]], axis=0)
    total = rows + above + below

    extent = place_ref[2]
    place_y = place_ref[0] + lax.broadcasted_iota(jnp.int32, (edge, edge, 1), 0)
    place_x = place_ref[1] + lax.broadcasted_iota(jnp.int32, (edge, edge, 1), 1)

    def line(place):
        return 1.0 + (place > 0).astype(F32) + (place < extent - 1).astype(F32)

    share = 1.0 / (line(place_y) * line(place_x))
    smoothed = (total * share).reshape(patches, LANES)[:, :classes]
    student = student_ref[image][:, :classes]

    top_t = jnp.max(smoothed, axis=-1, keepdims=True)
    expo_t = jnp.exp(smoothed - top_t)
    sum_t = jnp.sum(expo_t, axis=-1, keepdims=True)
    gap = jnp.sum(expo_t * (smoothed - student), axis=-1, keepdims=True)
    top_t, sum_t, gap = in_lanes([top_t, sum_t, gap])
    lse_s = lse_ref[pl.ds(image, 1), :]
    for k, stat in enumerate((top_t + jnp.log(sum_t), gap / sum_t, lse_s)):
        for c in range(parts):
            out_ref[c, pl.ds(k * images + image, 1), :] = stat


def patch_stats(place, student, lse_s, logits, borders, classes, parts):
    images, patches, _ = logits.shape
    edge = borders[0].shape[1]
    whole = pl.BlockSpec(memory_space=pltpu.VMEM)
    return pl.pallas_call(
        lambda *refs: stats_kernel(edge, classes, parts, images, *refs),
        grid=(images,),
        in_specs=[pl.BlockSpec(memory_space=pltpu.SMEM)] + [whole] * 7,
        out_specs=whole,
        out_shape=jax.ShapeDtypeStruct((parts, 3 * images, patches), F32),
        compiler_params=pltpu.CompilerParams(vmem_limit_bytes=16 * 2**20),
        cost_estimate=pl.CostEstimate(
            flops=30 * images * patches * LANES,
            bytes_accessed=2 * images * patches * LANES * 4,
            transcendentals=images * patches * LANES,
        ),
        name="patch_stats",
    )(place, student, lse_s, logits, *borders)


def divergence_kernel(images, tiles, stats_ref, valid_ref, divergence_ref, totals_ref):
    lse_t = stats_ref[:, :images, :]
    gap = stats_ref[:, images : 2 * images, :]
    lse_s = stats_ref[:, 2 * images :, :]
    top_t = jnp.max(lse_t, axis=0)
    top_s = jnp.max(lse_s, axis=0)
    share = jnp.exp(lse_t - top_t[None])
    sum_t = jnp.sum(share, axis=0)
    sum_s = jnp.sum(jnp.exp(lse_s - top_s[None]), axis=0)
    mean_gap = jnp.sum(share * gap, axis=0) / sum_t
    divergence = mean_gap - top_t - jnp.log(sum_t) + top_s + jnp.log(sum_s)
    divergence_ref[...] = divergence
    weights = valid_ref[...].astype(F32)
    total = jnp.sum(divergence * weights, axis=1, keepdims=True)
    number = jnp.sum(weights, axis=1, keepdims=True)
    shape = (images, 128)
    lane = lax.broadcasted_iota(jnp.int32, shape, 1)
    row = lax.broadcasted_iota(jnp.int32, shape, 0)
    both = jnp.where(lane == row, total, jnp.where(lane == row + images, number, 0.0))
    line = jnp.sum(both, axis=0, keepdims=True)
    totals_ref[...] = jnp.broadcast_to(line[None], totals_ref.shape)


def patch_divergence(stats, valid, tiles):
    images, patches = valid.shape
    whole = pl.BlockSpec(memory_space=pltpu.VMEM)
    return pl.pallas_call(
        lambda *refs: divergence_kernel(images, tiles, *refs),
        in_specs=[whole, whole],
        out_specs=[whole, whole],
        out_shape=[
            jax.ShapeDtypeStruct((images, patches), F32),
            jax.ShapeDtypeStruct((tiles, 1, 128), F32),
        ],
        compiler_params=pltpu.CompilerParams(vmem_limit_bytes=8 * 2**20),
        name="patch_divergence",
    )(stats, valid)


def everywhere_sum(x, tiles, parts):
    groups = []
    for start in range(parts):
        groups.append([t * parts + (start + t % 2 * (parts // 2)) % parts for t in range(tiles)])
    everyone = lax.all_to_all(
        x, ("space", "mp"), split_axis=0, concat_axis=0, tiled=True, axis_index_groups=groups
    )
    return jnp.sum(everyone, axis=(0, 1))


def body(teacher_tokens, student_tokens, teacher_head, student_head, valid):
    tiles = lax.axis_size("space")
    parts = lax.axis_size("mp")
    side = math.isqrt(tiles)
    tile_index = lax.axis_index("space")
    row, column = tile_index // side, tile_index % side
    images, _, edge, _, _ = teacher_tokens.shape
    classes = teacher_head.shape[1]
    flags = valid.reshape(images, edge * edge)
    place = jnp.stack([row * edge, column * edge, side * edge, 1 - row % 2, 1 - column % 2]).astype(jnp.int32)

    head_t, head_s = gathered_heads(teacher_head, student_head, tiles)
    logits, row_a, row_b, column_a, column_b = teacher_logits(place, teacher_tokens, head_t)
    column_b = swapped(column_b, pairs_of(side, 1, 0, 1), parts, 0)
    column_a = swapped(column_a, pairs_of(side, 0, 0, 1), parts, 0)
    row_a, row_b = row_sums(place, row_a, row_b, column_a, column_b)
    row_a = swapped(row_a, pairs_of(side, 0, 1, 0), parts, 0)
    row_b = swapped(row_b, pairs_of(side, 1, 1, 0), parts, 0)
    student, lse_s = student_logits(student_tokens, head_s, classes)
    stats = patch_stats(place, student, lse_s, logits, [row_a, row_b, column_a, column_b], classes, parts)
    stats = exchange(stats, "mp")
    divergence, totals = patch_divergence(stats, flags, tiles)
    totals = everywhere_sum(totals, tiles, parts)
    image_loss = totals[:images] / jnp.maximum(totals[images : 2 * images], 1.0)
    return (divergence.reshape(images, 1, edge, edge), image_loss)


def solution(mesh):
    in_specs = (
        P("dp", "space", None, None, None),
        P("dp", "space", None, None, None),
        P(("dp", "space"), "mp"),
        P(("dp", "space"), "mp"),
        P("dp", "space", None, None),
    )
    out_specs = (P("dp", "space", None, None), P("dp"))
    return jax.shard_map(body, mesh=mesh, in_specs=in_specs, out_specs=out_specs, check_vma=False)
```

```python
import math

import jax
import jax.numpy as jnp
from jax import lax
from jax.experimental import pallas as pl
from jax.experimental.pallas import tpu as pltpu
from jax.sharding import PartitionSpec as P

F32 = jnp.float32
LANES = 256
BLOCK = 4


def copies(x, count):
    return jnp.broadcast_to(x, (count, *x.shape))


def exchange(x, axis):
    return lax.all_to_all(x, axis, split_axis=0, concat_axis=0, tiled=True)


def padded(head):
    return jnp.pad(head, ((0, 0), (0, LANES - head.shape[1])))


def gathered_heads(teacher_head, student_head, tiles):
    cut = teacher_head.shape[0]
    own = padded(jnp.concatenate([teacher_head, student_head]))
    other = lax.ppermute(own, "space", [(t, t ^ 1) for t in range(tiles)])
    is_even = lax.axis_index("space") % 2 == 0
    even, odd = jnp.where(is_even, own, other), jnp.where(is_even, other, own)
    groups = [list(range(z, tiles, 2)) for z in range(2)]

    def along_y(pair):
        return lax.all_to_all(pair, "space", split_axis=0, concat_axis=0, tiled=True, axis_index_groups=groups)

    first = along_y(copies(jnp.concatenate([even[:cut], odd[:cut]]), tiles // 2))
    second = copies(jnp.concatenate([even[cut:], odd[cut:]]), tiles // 2)
    second, first = lax.optimization_barrier((second, first))
    second = along_y(second)
    return first.reshape(-1, LANES), second.reshape(-1, LANES)


def swapped(block, pairs, parts, shift):
    route = []
    for a, b in pairs:
        for m in range(parts):
            n = (m + shift) % parts
            route += [(a * parts + m, b * parts + n), (b * parts + n, a * parts + m)]
    return lax.ppermute(block, ("space", "mp"), route)


def pairs_of(side, start, down, right):
    pairs = []
    for row in range(side):
        for column in range(side):
            place = row * down + column * right
            if place % 2 == start and place + 1 < side:
                here = row * side + column
                pairs.append((here, here + down * side + right))
    return pairs


def in_lanes(columns):
    height = columns[0].shape[0]
    lane = lax.broadcasted_iota(jnp.int32, (height, 128), 1)
    packed = jnp.broadcast_to(columns[-1], (height, 128))
    for k, column in enumerate(columns[:-1]):
        packed = jnp.where(lane == k, column, packed)
    rows = packed.T
    return [rows[k : k + 1] for k in range(len(columns))]


def teacher_kernel(block, place_ref, tokens_ref, head_ref, logits_ref, row_a, row_b, column_a, column_b):
    edge, width = tokens_ref.shape[2], tokens_ref.shape[-1]
    images, patches, _ = logits_ref.shape
    row_even, column_even = place_ref[3] == 1, place_ref[4] == 1
    for start in range(0, images, block):
        tokens = tokens_ref[start : start + block, 0].reshape(block * patches, width)
        logits = jnp.dot(tokens, head_ref[...], preferred_element_type=F32)
        for i in range(block):
            image = logits[i * patches : (i + 1) * patches]
            logits_ref[start + i] = image
            cube = image.reshape(edge, edge, LANES)
            first, last = cube[0], cube[edge - 1]
            row_a[start + i] = jnp.where(row_even, last, first)
            row_b[start + i] = jnp.where(row_even, first, last)
            left, right = cube[:, 0, :], cube[:, edge - 1, :]
            column_a[start + i] = jnp.where(column_even, right, left)
            column_b[start + i] = jnp.where(column_even, left, right)


def teacher_logits(place, tokens, head):
    images, _, edge, _, width = tokens.shape
    patches = edge * edge
    border = jax.ShapeDtypeStruct((images, edge, LANES), F32)
    whole = pl.BlockSpec(memory_space=pltpu.VMEM)
    return pl.pallas_call(
        lambda *refs: teacher_kernel(math.gcd(images, BLOCK), *refs),
        in_specs=[pl.BlockSpec(memory_space=pltpu.SMEM), whole, whole],
        out_specs=[whole] * 5,
        out_shape=[jax.ShapeDtypeStruct((images, patches, LANES), F32)] + [border] * 4,
        compiler_params=pltpu.CompilerParams(vmem_limit_bytes=16 * 2**20),
        cost_estimate=pl.CostEstimate(
            flops=2 * images * patches * width * LANES,
            bytes_accessed=tokens.size * 2 + head.size * 2 + images * patches * LANES * 4,
            transcendentals=0,
        ),
        name="teacher_logits",
    )(place, tokens, head)


def row_kernel(place_ref, row_a, row_b, column_a, column_b, out_a, out_b):
    images, edge, _ = row_a.shape
    row_even, column_even = place_ref[3] == 1, place_ref[4] == 1
    left = jnp.where(column_even, column_b[...], column_a[...])
    right = jnp.where(column_even, column_a[...], column_b[...])
    x = lax.broadcasted_iota(jnp.int32, (edge, LANES), 0)
    for row, out, at_end in ((row_a, out_a, row_even), (row_b, out_b, ~row_even)):
        for i in range(images):
            line = row[i]
            start = jnp.where(at_end, left[i, edge - 1 :], left[i, :1])
            end = jnp.where(at_end, right[i, edge - 1 :], right[i, :1])
            before = jnp.where(x == 0, start, pltpu.roll(line, 1, 0))
            after = jnp.where(x == edge - 1, end, pltpu.roll(line, edge - 1, 0))
            out[i] = line + before + after


def row_sums(place, row_a, row_b, column_a, column_b):
    whole = pl.BlockSpec(memory_space=pltpu.VMEM)
    return pl.pallas_call(
        row_kernel,
        in_specs=[pl.BlockSpec(memory_space=pltpu.SMEM)] + [whole] * 4,
        out_specs=[whole] * 2,
        out_shape=[jax.ShapeDtypeStruct(row_a.shape, F32)] * 2,
        compiler_params=pltpu.CompilerParams(vmem_limit_bytes=4 * 2**20),
        cost_estimate=pl.CostEstimate(flops=10 * row_a.size, bytes_accessed=24 * row_a.size, transcendentals=0),
        name="row_sums",
    )(place, row_a, row_b, column_a, column_b)


def student_kernel(block, classes, tokens_ref, head_ref, logits_ref, lse_ref):
    images, patches, _ = logits_ref.shape
    for start in range(0, images, block):
        tokens = tokens_ref[start : start + block, 0].reshape(block * patches, tokens_ref.shape[-1])
        logits = jnp.dot(tokens, head_ref[...], preferred_element_type=F32)
        for i in range(block):
            image = logits[i * patches : (i + 1) * patches]
            logits_ref[start + i] = image
            image = image[:, :classes]
            top = jnp.max(image, axis=-1, keepdims=True)
            total = jnp.sum(jnp.exp(image - top), axis=-1, keepdims=True)
            top, total = in_lanes([top, total])
            lse_ref[start + i : start + i + 1, :] = top + jnp.log(total)


def student_logits(tokens, head, classes):
    images, _, edge, _, width = tokens.shape
    patches = edge * edge
    whole = pl.BlockSpec(memory_space=pltpu.VMEM)
    return pl.pallas_call(
        lambda *refs: student_kernel(math.gcd(images, BLOCK), classes, *refs),
        in_specs=[whole, whole],
        out_specs=[whole, whole],
        out_shape=[
            jax.ShapeDtypeStruct((images, patches, LANES), F32),
            jax.ShapeDtypeStruct((images, patches), F32),
        ],
        compiler_params=pltpu.CompilerParams(vmem_limit_bytes=16 * 2**20),
        cost_estimate=pl.CostEstimate(
            flops=2 * images * patches * width * LANES,
            bytes_accessed=tokens.size * 2 + head.size * 2 + images * patches * LANES * 4,
            transcendentals=images * patches * LANES,
        ),
        name="student_logits",
    )(tokens, head)


def stats_kernel(
    edge,
    classes,
    parts,
    images,
    place_ref,
    student_ref,
    lse_ref,
    logits_ref,
    row_a,
    row_b,
    column_a,
    column_b,
    out_ref,
    share_ref,
):
    image = pl.program_id(0)
    patches = edge * edge
    shape = (edge, edge, LANES)
    row_even, column_even = place_ref[3] == 1, place_ref[4] == 1

    flat = logits_ref[image]
    cube = flat.reshape(shape)
    half = edge // 2
    x = lax.broadcasted_iota(jnp.int32, (edge, half, LANES), 1)
    to_left = jnp.where(column_even, column_b[image], column_a[image])[:, None, :]
    to_right = jnp.where(column_even, column_a[image], column_b[image])[:, None, :]
    before = pltpu.roll(flat, 1, 0).reshape(shape)
    before = jnp.concatenate([jnp.where(x == 0, to_left, before[:, :half]), before[:, half:]], axis=1)
    after = pltpu.roll(flat, patches - 1, 0).reshape(shape)
    after = jnp.concatenate([after[:, :half], jnp.where(x == half - 1, to_right, after[:, half:])], axis=1)
    rows = cube + before + after
    up = jnp.where(row_even, row_b[image], row_a[image])
    down = jnp.where(row_even, row_a[image], row_b[image])
    above = jnp.concatenate([up[None], rows[:-1]], axis=0)
    below = jnp.concatenate([rows[1:], down[None]], axis=0)
    total = rows + above + below

    @pl.when(image == 0)
    def _():
        extent = place_ref[2]
        place_y = place_ref[0] + lax.broadcasted_iota(jnp.int32, shape, 0)
        place_x = place_ref[1] + lax.broadcasted_iota(jnp.int32, shape, 1)

        def line(place):
            return 1.0 + (place > 0).astype(F32) + (place < extent - 1).astype(F32)

        share_ref[...] = (1.0 / (line(place_y) * line(place_x))).reshape(patches, LANES)

    smoothed = (total.reshape(patches, LANES) * share_ref[...])[:, :classes]
    student = student_ref[image][:, :classes]

    top_t = jnp.max(smoothed, axis=-1, keepdims=True)
    expo_t = jnp.exp(smoothed - top_t)
    sum_t = jnp.sum(expo_t, axis=-1, keepdims=True)
    gap = jnp.sum(expo_t * (smoothed - student), axis=-1, keepdims=True)
    top_t, sum_t, gap = in_lanes([top_t, sum_t, gap])
    lse_s = lse_ref[pl.ds(image, 1), :]
    for k, stat in enumerate((top_t + jnp.log(sum_t), gap / sum_t, lse_s)):
        for c in range(parts):
            out_ref[c, pl.ds(k * images + image, 1), :] = stat


def patch_stats(place, student, lse_s, logits, borders, classes, parts):
    images, patches, _ = logits.shape
    edge = borders[0].shape[1]
    whole = pl.BlockSpec(memory_space=pltpu.VMEM)
    return pl.pallas_call(
        lambda *refs: stats_kernel(edge, classes, parts, images, *refs),
        grid=(images,),
        in_specs=[pl.BlockSpec(memory_space=pltpu.SMEM)] + [whole] * 7,
        out_specs=whole,
        out_shape=jax.ShapeDtypeStruct((parts, 3 * images, patches), F32),
        scratch_shapes=[pltpu.VMEM((patches, LANES), F32)],
        compiler_params=pltpu.CompilerParams(vmem_limit_bytes=16 * 2**20),
        cost_estimate=pl.CostEstimate(
            flops=30 * images * patches * LANES,
            bytes_accessed=2 * images * patches * LANES * 4,
            transcendentals=images * patches * LANES,
        ),
        name="patch_stats",
    )(place, student, lse_s, logits, *borders)


def divergence_kernel(images, tiles, stats_ref, valid_ref, divergence_ref, totals_ref):
    lse_t = stats_ref[:, :images, :]
    gap = stats_ref[:, images : 2 * images, :]
    lse_s = stats_ref[:, 2 * images :, :]
    top_t = jnp.max(lse_t, axis=0)
    top_s = jnp.max(lse_s, axis=0)
    share = jnp.exp(lse_t - top_t[None])
    sum_t = jnp.sum(share, axis=0)
    sum_s = jnp.sum(jnp.exp(lse_s - top_s[None]), axis=0)
    mean_gap = jnp.sum(share * gap, axis=0) / sum_t
    divergence = mean_gap - top_t - jnp.log(sum_t) + top_s + jnp.log(sum_s)
    divergence_ref[...] = divergence
    weights = valid_ref[...].astype(F32)
    total = jnp.sum(divergence * weights, axis=1, keepdims=True)
    number = jnp.sum(weights, axis=1, keepdims=True)
    shape = (images, 128)
    lane = lax.broadcasted_iota(jnp.int32, shape, 1)
    row = lax.broadcasted_iota(jnp.int32, shape, 0)
    both = jnp.where(lane == row, total, jnp.where(lane == row + images, number, 0.0))
    line = jnp.sum(both, axis=0, keepdims=True)
    totals_ref[...] = jnp.broadcast_to(line[None], totals_ref.shape)


def patch_divergence(stats, valid, tiles):
    images, patches = valid.shape
    whole = pl.BlockSpec(memory_space=pltpu.VMEM)
    return pl.pallas_call(
        lambda *refs: divergence_kernel(images, tiles, *refs),
        in_specs=[whole, whole],
        out_specs=[whole, whole],
        out_shape=[
            jax.ShapeDtypeStruct((images, patches), F32),
            jax.ShapeDtypeStruct((tiles, 1, 128), F32),
        ],
        compiler_params=pltpu.CompilerParams(vmem_limit_bytes=8 * 2**20),
        name="patch_divergence",
    )(stats, valid)


def everywhere_sum(x, tiles, parts):
    groups = []
    for start in range(parts):
        groups.append([t * parts + (start + t % 2 * (parts // 2)) % parts for t in range(tiles)])
    everyone = lax.all_to_all(
        x, ("space", "mp"), split_axis=0, concat_axis=0, tiled=True, axis_index_groups=groups
    )
    return jnp.sum(everyone, axis=(0, 1))


def body(teacher_tokens, student_tokens, teacher_head, student_head, valid):
    tiles = lax.axis_size("space")
    parts = lax.axis_size("mp")
    side = math.isqrt(tiles)
    tile_index = lax.axis_index("space")
    row, column = tile_index // side, tile_index % side
    images, _, edge, _, _ = teacher_tokens.shape
    classes = teacher_head.shape[1]
    flags = valid.reshape(images, edge * edge)
    place = jnp.stack([row * edge, column * edge, side * edge, 1 - row % 2, 1 - column % 2]).astype(jnp.int32)

    head_t, head_s = gathered_heads(teacher_head, student_head, tiles)
    logits, row_a, row_b, column_a, column_b = teacher_logits(place, teacher_tokens, head_t)
    column_b = swapped(column_b, pairs_of(side, 1, 0, 1), parts, 0)
    column_a = swapped(column_a, pairs_of(side, 0, 0, 1), parts, 0)
    row_a, row_b = row_sums(place, row_a, row_b, column_a, column_b)
    row_a = swapped(row_a, pairs_of(side, 0, 1, 0), parts, 0)
    row_b = swapped(row_b, pairs_of(side, 1, 1, 0), parts, 0)
    student, lse_s = student_logits(student_tokens, head_s, classes)
    stats = patch_stats(place, student, lse_s, logits, [row_a, row_b, column_a, column_b], classes, parts)
    stats = exchange(stats, "mp")
    divergence, totals = patch_divergence(stats, flags, tiles)
    totals = everywhere_sum(totals, tiles, parts)
    image_loss = totals[:images] / jnp.maximum(totals[images : 2 * images], 1.0)
    return (divergence.reshape(images, 1, edge, edge), image_loss)


def solution(mesh):
    in_specs = (
        P("dp", "space", None, None, None),
        P("dp", "space", None, None, None),
        P(("dp", "space"), "mp"),
        P(("dp", "space"), "mp"),
        P("dp", "space", None, None),
    )
    out_specs = (P("dp", "space", None, None), P("dp"))
    return jax.shard_map(body, mesh=mesh, in_specs=in_specs, out_specs=out_specs, check_vma=False)
```

```python
import math

import jax
import jax.numpy as jnp
from jax import lax
from jax.experimental import pallas as pl
from jax.experimental.pallas import tpu as pltpu
from jax.sharding import PartitionSpec as P

F32 = jnp.float32
LANES = 256
BLOCK = 4


def copies(x, count):
    return jnp.broadcast_to(x, (count, *x.shape))


def exchange(x, axis):
    return lax.all_to_all(x, axis, split_axis=0, concat_axis=0, tiled=True)


def padded(head):
    return jnp.pad(head, ((0, 0), (0, LANES - head.shape[1])))


def gathered_heads(teacher_head, student_head, tiles):
    cut = teacher_head.shape[0]
    own = padded(jnp.concatenate([teacher_head, student_head]))
    other = lax.ppermute(own, "space", [(t, t ^ 1) for t in range(tiles)])
    is_even = lax.axis_index("space") % 2 == 0
    even, odd = jnp.where(is_even, own, other), jnp.where(is_even, other, own)
    groups = [list(range(z, tiles, 2)) for z in range(2)]

    def along_y(pair):
        return lax.all_to_all(pair, "space", split_axis=0, concat_axis=0, tiled=True, axis_index_groups=groups)

    first = along_y(copies(jnp.concatenate([even[:cut], odd[:cut]]), tiles // 2))
    second = copies(jnp.concatenate([even[cut:], odd[cut:]]), tiles // 2)
    second, first = lax.optimization_barrier((second, first))
    second = along_y(second)
    return first.reshape(-1, LANES), second.reshape(-1, LANES)


def swapped(block, pairs, parts, shift):
    route = []
    for a, b in pairs:
        for m in range(parts):
            n = (m + shift) % parts
            route += [(a * parts + m, b * parts + n), (b * parts + n, a * parts + m)]
    return lax.ppermute(block, ("space", "mp"), route)


def pairs_of(side, start, down, right):
    pairs = []
    for row in range(side):
        for column in range(side):
            place = row * down + column * right
            if place % 2 == start and place + 1 < side:
                here = row * side + column
                pairs.append((here, here + down * side + right))
    return pairs


def in_lanes(columns):
    height = columns[0].shape[0]
    lane = lax.broadcasted_iota(jnp.int32, (height, 128), 1)
    packed = jnp.broadcast_to(columns[-1], (height, 128))
    for k, column in enumerate(columns[:-1]):
        packed = jnp.where(lane == k, column, packed)
    rows = packed.T
    return [rows[k : k + 1] for k in range(len(columns))]


def teacher_kernel(block, place_ref, tokens_ref, head_ref, logits_ref, row_a, row_b, column_a, column_b):
    edge, width = tokens_ref.shape[2], tokens_ref.shape[-1]
    images, patches, _ = logits_ref.shape
    row_even, column_even = place_ref[3] == 1, place_ref[4] == 1
    for start in range(0, images, block):
        tokens = tokens_ref[start : start + block, 0].reshape(block * patches, width)
        logits = jnp.dot(tokens, head_ref[...], preferred_element_type=F32)
        for i in range(block):
            image = logits[i * patches : (i + 1) * patches]
            logits_ref[start + i] = image
            cube = image.reshape(edge, edge, LANES)
            first, last = cube[0], cube[edge - 1]
            row_a[start + i] = jnp.where(row_even, last, first)
            row_b[start + i] = jnp.where(row_even, first, last)
            left, right = cube[:, 0, :], cube[:, edge - 1, :]
            column_a[start + i] = jnp.where(column_even, right, left)
            column_b[start + i] = jnp.where(column_even, left, right)


def teacher_logits(place, tokens, head):
    images, _, edge, _, width = tokens.shape
    patches = edge * edge
    border = jax.ShapeDtypeStruct((images, edge, LANES), F32)
    whole = pl.BlockSpec(memory_space=pltpu.VMEM)
    return pl.pallas_call(
        lambda *refs: teacher_kernel(math.gcd(images, BLOCK), *refs),
        in_specs=[pl.BlockSpec(memory_space=pltpu.SMEM), whole, whole],
        out_specs=[whole] * 5,
        out_shape=[jax.ShapeDtypeStruct((images, patches, LANES), F32)] + [border] * 4,
        compiler_params=pltpu.CompilerParams(vmem_limit_bytes=16 * 2**20),
        cost_estimate=pl.CostEstimate(
            flops=2 * images * patches * width * LANES,
            bytes_accessed=tokens.size * 2 + head.size * 2 + images * patches * LANES * 4,
            transcendentals=0,
        ),
        name="teacher_logits",
    )(place, tokens, head)


def row_kernel(place_ref, row_a, row_b, column_a, column_b, out_a, out_b):
    images, edge, _ = row_a.shape
    row_even, column_even = place_ref[3] == 1, place_ref[4] == 1
    left = jnp.where(column_even, column_b[...], column_a[...])
    right = jnp.where(column_even, column_a[...], column_b[...])
    x = lax.broadcasted_iota(jnp.int32, (edge, LANES), 0)
    for row, out, at_end in ((row_a, out_a, row_even), (row_b, out_b, ~row_even)):
        for i in range(images):
            line = row[i]
            start = jnp.where(at_end, left[i, edge - 1 :], left[i, :1])
            end = jnp.where(at_end, right[i, edge - 1 :], right[i, :1])
            before = jnp.where(x == 0, start, pltpu.roll(line, 1, 0))
            after = jnp.where(x == edge - 1, end, pltpu.roll(line, edge - 1, 0))
            out[i] = line + before + after


def row_sums(place, row_a, row_b, column_a, column_b):
    whole = pl.BlockSpec(memory_space=pltpu.VMEM)
    return pl.pallas_call(
        row_kernel,
        in_specs=[pl.BlockSpec(memory_space=pltpu.SMEM)] + [whole] * 4,
        out_specs=[whole] * 2,
        out_shape=[jax.ShapeDtypeStruct(row_a.shape, F32)] * 2,
        compiler_params=pltpu.CompilerParams(vmem_limit_bytes=4 * 2**20),
        cost_estimate=pl.CostEstimate(flops=10 * row_a.size, bytes_accessed=24 * row_a.size, transcendentals=0),
        name="row_sums",
    )(place, row_a, row_b, column_a, column_b)


def student_kernel(block, classes, tokens_ref, head_ref, logits_ref, lse_ref):
    images, patches, _ = logits_ref.shape
    for start in range(0, images, block):
        tokens = tokens_ref[start : start + block, 0].reshape(block * patches, tokens_ref.shape[-1])
        logits = jnp.dot(tokens, head_ref[...], preferred_element_type=F32)
        for i in range(block):
            image = logits[i * patches : (i + 1) * patches]
            logits_ref[start + i] = image
            image = image[:, :classes]
            top = jnp.max(image, axis=-1, keepdims=True)
            total = jnp.sum(jnp.exp(image - top), axis=-1, keepdims=True)
            top, total = in_lanes([top, total])
            lse_ref[start + i : start + i + 1, :] = top + jnp.log(total)


def student_logits(tokens, head, classes):
    images, _, edge, _, width = tokens.shape
    patches = edge * edge
    whole = pl.BlockSpec(memory_space=pltpu.VMEM)
    return pl.pallas_call(
        lambda *refs: student_kernel(math.gcd(images, BLOCK), classes, *refs),
        in_specs=[whole, whole],
        out_specs=[whole, whole],
        out_shape=[
            jax.ShapeDtypeStruct((images, patches, LANES), F32),
            jax.ShapeDtypeStruct((images, patches), F32),
        ],
        compiler_params=pltpu.CompilerParams(vmem_limit_bytes=16 * 2**20),
        cost_estimate=pl.CostEstimate(
            flops=2 * images * patches * width * LANES,
            bytes_accessed=tokens.size * 2 + head.size * 2 + images * patches * LANES * 4,
            transcendentals=images * patches * LANES,
        ),
        name="student_logits",
    )(tokens, head)


def stats_kernel(
    edge,
    classes,
    parts,
    images,
    place_ref,
    student_ref,
    lse_ref,
    logits_ref,
    row_a,
    row_b,
    column_a,
    column_b,
    out_ref,
    share_ref,
):
    patches = edge * edge
    shape = (edge, edge, LANES)
    row_even, column_even = place_ref[3] == 1, place_ref[4] == 1

    extent = place_ref[2]
    place_y = place_ref[0] + lax.broadcasted_iota(jnp.int32, shape, 0)
    place_x = place_ref[1] + lax.broadcasted_iota(jnp.int32, shape, 1)

    def line(place):
        return 1.0 + (place > 0).astype(F32) + (place < extent - 1).astype(F32)

    share_ref[...] = (1.0 / (line(place_y) * line(place_x))).reshape(patches, LANES)

    half = edge // 2
    x = lax.broadcasted_iota(jnp.int32, (edge, half, LANES), 1)
    for image in range(images):
        flat = logits_ref[image]
        cube = flat.reshape(shape)
        to_left = jnp.where(column_even, column_b[image], column_a[image])[:, None, :]
        to_right = jnp.where(column_even, column_a[image], column_b[image])[:, None, :]
        before = pltpu.roll(flat, 1, 0).reshape(shape)
        before = jnp.concatenate([jnp.where(x == 0, to_left, before[:, :half]), before[:, half:]], axis=1)
        after = pltpu.roll(flat, patches - 1, 0).reshape(shape)
        after = jnp.concatenate([after[:, :half], jnp.where(x == half - 1, to_right, after[:, half:])], axis=1)
        rows = cube + before + after
        up = jnp.where(row_even, row_b[image], row_a[image])
        down = jnp.where(row_even, row_a[image], row_b[image])
        above = jnp.concatenate([up[None], rows[:-1]], axis=0)
        below = jnp.concatenate([rows[1:], down[None]], axis=0)
        total = rows + above + below

        smoothed = (total.reshape(patches, LANES) * share_ref[...])[:, :classes]
        student = student_ref[image][:, :classes]

        top_t = jnp.max(smoothed, axis=-1, keepdims=True)
        expo_t = jnp.exp(smoothed - top_t)
        sum_t = jnp.sum(expo_t, axis=-1, keepdims=True)
        gap = jnp.sum(expo_t * (smoothed - student), axis=-1, keepdims=True)
        top_t, sum_t, gap = in_lanes([top_t, sum_t, gap])
        lse_s = lse_ref[image : image + 1, :]
        for k, stat in enumerate((top_t + jnp.log(sum_t), gap / sum_t, lse_s)):
            for c in range(parts):
                out_ref[c, k * images + image : k * images + image + 1, :] = stat


def patch_stats(place, student, lse_s, logits, borders, classes, parts):
    images, patches, _ = logits.shape
    edge = borders[0].shape[1]
    whole = pl.BlockSpec(memory_space=pltpu.VMEM)
    return pl.pallas_call(
        lambda *refs: stats_kernel(edge, classes, parts, images, *refs),
        in_specs=[pl.BlockSpec(memory_space=pltpu.SMEM)] + [whole] * 7,
        out_specs=whole,
        out_shape=jax.ShapeDtypeStruct((parts, 3 * images, patches), F32),
        scratch_shapes=[pltpu.VMEM((patches, LANES), F32)],
        compiler_params=pltpu.CompilerParams(vmem_limit_bytes=16 * 2**20),
        cost_estimate=pl.CostEstimate(
            flops=30 * images * patches * LANES,
            bytes_accessed=2 * images * patches * LANES * 4,
            transcendentals=images * patches * LANES,
        ),
        name="patch_stats",
    )(place, student, lse_s, logits, *borders)


def divergence_kernel(images, tiles, stats_ref, valid_ref, divergence_ref, totals_ref):
    lse_t = stats_ref[:, :images, :]
    gap = stats_ref[:, images : 2 * images, :]
    lse_s = stats_ref[:, 2 * images :, :]
    top_t = jnp.max(lse_t, axis=0)
    top_s = jnp.max(lse_s, axis=0)
    share = jnp.exp(lse_t - top_t[None])
    sum_t = jnp.sum(share, axis=0)
    sum_s = jnp.sum(jnp.exp(lse_s - top_s[None]), axis=0)
    mean_gap = jnp.sum(share * gap, axis=0) / sum_t
    divergence = mean_gap - top_t - jnp.log(sum_t) + top_s + jnp.log(sum_s)
    divergence_ref[...] = divergence
    weights = valid_ref[...].astype(F32)
    total = jnp.sum(divergence * weights, axis=1, keepdims=True)
    number = jnp.sum(weights, axis=1, keepdims=True)
    shape = (images, 128)
    lane = lax.broadcasted_iota(jnp.int32, shape, 1)
    row = lax.broadcasted_iota(jnp.int32, shape, 0)
    both = jnp.where(lane == row, total, jnp.where(lane == row + images, number, 0.0))
    line = jnp.sum(both, axis=0, keepdims=True)
    totals_ref[...] = jnp.broadcast_to(line[None], totals_ref.shape)


def patch_divergence(stats, valid, tiles):
    images, patches = valid.shape
    whole = pl.BlockSpec(memory_space=pltpu.VMEM)
    return pl.pallas_call(
        lambda *refs: divergence_kernel(images, tiles, *refs),
        in_specs=[whole, whole],
        out_specs=[whole, whole],
        out_shape=[
            jax.ShapeDtypeStruct((images, patches), F32),
            jax.ShapeDtypeStruct((tiles, 1, 128), F32),
        ],
        compiler_params=pltpu.CompilerParams(vmem_limit_bytes=8 * 2**20),
        name="patch_divergence",
    )(stats, valid)


def everywhere_sum(x, tiles, parts):
    groups = []
    for start in range(parts):
        groups.append([t * parts + (start + t % 2 * (parts // 2)) % parts for t in range(tiles)])
    everyone = lax.all_to_all(
        x, ("space", "mp"), split_axis=0, concat_axis=0, tiled=True, axis_index_groups=groups
    )
    return jnp.sum(everyone, axis=(0, 1))


def body(teacher_tokens, student_tokens, teacher_head, student_head, valid):
    tiles = lax.axis_size("space")
    parts = lax.axis_size("mp")
    side = math.isqrt(tiles)
    tile_index = lax.axis_index("space")
    row, column = tile_index // side, tile_index % side
    images, _, edge, _, _ = teacher_tokens.shape
    classes = teacher_head.shape[1]
    flags = valid.reshape(images, edge * edge)
    place = jnp.stack([row * edge, column * edge, side * edge, 1 - row % 2, 1 - column % 2]).astype(jnp.int32)

    head_t, head_s = gathered_heads(teacher_head, student_head, tiles)
    logits, row_a, row_b, column_a, column_b = teacher_logits(place, teacher_tokens, head_t)
    column_b = swapped(column_b, pairs_of(side, 1, 0, 1), parts, 0)
    column_a = swapped(column_a, pairs_of(side, 0, 0, 1), parts, 0)
    row_a, row_b = row_sums(place, row_a, row_b, column_a, column_b)
    row_a = swapped(row_a, pairs_of(side, 0, 1, 0), parts, 0)
    row_b = swapped(row_b, pairs_of(side, 1, 1, 0), parts, 0)
    student, lse_s = student_logits(student_tokens, head_s, classes)
    stats = patch_stats(place, student, lse_s, logits, [row_a, row_b, column_a, column_b], classes, parts)
    stats = exchange(stats, "mp")
    divergence, totals = patch_divergence(stats, flags, tiles)
    totals = everywhere_sum(totals, tiles, parts)
    image_loss = totals[:images] / jnp.maximum(totals[images : 2 * images], 1.0)
    return (divergence.reshape(images, 1, edge, edge), image_loss)


def solution(mesh):
    in_specs = (
        P("dp", "space", None, None, None),
        P("dp", "space", None, None, None),
        P(("dp", "space"), "mp"),
        P(("dp", "space"), "mp"),
        P("dp", "space", None, None),
    )
    out_specs = (P("dp", "space", None, None), P("dp"))
    return jax.shard_map(body, mesh=mesh, in_specs=in_specs, out_specs=out_specs, check_vma=False)
```
